128 devices in a mesh: tile: 32 (over y_lo, z, x), slab: 4 (over y_hi, core).
Axes of the slice: x: 4, y: 4 (y_hi: 2, y_lo: 2; y = y_hi * 2 + y_lo), z: 4, core: 2. Of those that a mesh axis runs over, the one named last changes fastest.
Arguments:
- pixels: bfloat16 [4, 128, 128, 384], P('slab', 'tile'), may hold values from -12 to 12
- tissue: int32 [4, 128, 1024], P('slab', 'tile'), may hold values from 0 to 1, as said below
- neighbours: int32 [4, 128, 8], P('slab', 'tile'), may hold values from -1 to 127, as said below
- upstream: bfloat16 [4, 128, 32, 3072], P('slab', 'tile'), may hold values from -6 to 6
- stem_weight: bfloat16 [48, 96], replicated, may hold values from -0.875 to 0.875
- stem_gain: float32 [96], replicated, may hold values from 0.5 to 1.5
- dw_weight: float32 [49, 96], replicated, may hold values from -1.8 to 1.8
- norm_gain: float32 [96], replicated, may hold values from 0.5 to 1.5
- up_weight: bfloat16 [96, 384], replicated, may hold values from -0.625 to 0.625
- down_weight: bfloat16 [384, 96], replicated, may hold values from -0.3125 to 0.3125
- layer_scale: float32 [96], replicated, may hold values from 0.2 to 1
Outputs:
- features: bfloat16 [4, 128, 32, 3072], P('slab', 'tile')
- grad_dw: float32 [49, 96], replicated
- grad_gain: float32 [96], replicated
- grad_up: float32 [96, 384], replicated
- grad_down: float32 [384, 96], replicated
- grad_scale: float32 [96], replicated
The draws below stay inside these ranges and needn't reach their ends.
Inputs may be any that keep to these rules, and one draw needn't show every extreme that they name: `neighbours`: for each tile slot, the slot (numbered within its region, device by device along tile) of the tissue tile beside it to the north, south, west, east, north-west, north-east, south-west and south-east, or -1 where there is none; -1 throughout in slots that hold no tile; the relation is symmetric. A region's tiles are numbered down the columns of a band 4 tiles high (the first tile may stand at any row of its band) and the devices of the region take them in order, each 1 to 4 consecutive tiles in its first slots; some device holds 4. So a tile beside a tile lies at most 5 devices away along tile, and in every region some lies exactly that far. 1 on cells that lie on tissue; all zero in slots that hold no tile.
All inputs are finite; a program needn't handle non-finite values.
Results may differ from the reference program's by a relative error of at most 0.0083.
Values may be sent and summed in bfloat16 or wider, within the bound.
A program may use at most 128 MiB of HBM per device.

```python
import math
import jax
import jax.numpy as jnp
from jax import lax

C = 96
HID = 384
PX = 128
PATCH = 4
KS = 7
SLOTS = 4
BAND = 4
SIDE = 32
CELLS = 1024
RIM = 3
REGIONS = 4
REGION_SLOTS = 128
N_TILE = 32
N_SLAB = 4


def balance(key):
    inner_key = jax.random.fold_in(key, 101)
    level_key, run_key, flip_key, shift_key = jax.random.split(inner_key, 4)
    devices = REGION_SLOTS // SLOTS
    level_draw = jax.random.randint(level_key, (REGIONS, devices), 0, SLOTS + 4)
    tile_loads = jnp.clip(level_draw - 3, 1, SLOTS)
    segment = jax.random.randint(run_key, (REGIONS, 1), 0, devices - 7)
    flipped = jax.random.randint(flip_key, (REGIONS, 1), 0, 2)
    run_start = segment + flipped
    big_device = segment + 7 * (1 - flipped)
    device = jnp.arange(devices, dtype=jnp.int32)[None, :]
    tile_loads = jnp.where((device >= run_start) & (device < run_start + 7), 1, tile_loads)
    tile_loads = jnp.where(device == big_device, SLOTS, tile_loads)
    starts = jnp.cumsum(tile_loads, axis=1) - tile_loads
    band_shift = jax.random.randint(shift_key, (REGIONS, 1), 0, BAND)
    return (tile_loads.astype(jnp.int32), starts.astype(jnp.int32), band_shift.astype(jnp.int32))


def tile_numbers(tile_loads, starts):
    slot_index = jnp.arange(REGION_SLOTS, dtype=jnp.int32)
    holder = slot_index // SLOTS
    within = slot_index - holder * SLOTS
    load_here = jnp.take(tile_loads, holder, axis=1)
    start_here = jnp.take(starts, holder, axis=1)
    occupied = within[None, :] < load_here
    number = jnp.where(occupied, start_here + within[None, :], -1)
    return (number, occupied)


def draw_neighbours(key, part):
    tile_loads, starts, band_shift = balance(key)
    number, occupied = tile_numbers(tile_loads, starts)
    devices = REGION_SLOTS // SLOTS
    tile_total = jnp.sum(tile_loads, axis=1)[:, None, None]
    band_row = ((jnp.maximum(number, 0) + band_shift) % BAND)[..., None]
    deltas = jnp.array([-1, 1, -BAND, BAND, -BAND - 1, BAND - 1, 1 - BAND, BAND + 1], jnp.int32)
    needs_above = jnp.array([1, 0, 0, 0, 1, 1, 0, 0], jnp.int32)
    needs_below = jnp.array([0, 1, 0, 0, 0, 0, 1, 1], jnp.int32)
    other_tile = number[..., None] + deltas
    exists = occupied[..., None] & (other_tile >= 0) & (other_tile < tile_total)
    exists = exists & ((needs_above == 0) | (band_row > 0)) & ((needs_below == 0) | (band_row < BAND - 1))
    clipped = jnp.maximum(other_tile, 0)
    holder = jnp.sum((starts[:, None, None, :] <= clipped[..., None]).astype(jnp.int32), axis=-1) - 1
    holder_match = holder[..., None] == jnp.arange(devices, dtype=jnp.int32)
    begin_tile = jnp.sum(jnp.where(holder_match, starts[:, None, None, :], 0), axis=-1)
    slot_found = holder * SLOTS + clipped - begin_tile
    return jnp.where(exists, slot_found, -1).astype(jnp.int32)


def draw_tissue(key, part):
    tile_loads, starts, band_shift = balance(key)
    key = jax.random.fold_in(key, 13)
    number, occupied = tile_numbers(tile_loads, starts)
    subkeys = jax.random.split(key, 4)
    tilt_rows = jax.random.randint(subkeys[0], (REGIONS, REGION_SLOTS, 1), -3, 4)
    tilt_cols = jax.random.randint(subkeys[1], (REGIONS, REGION_SLOTS, 1), -3, 4)
    offset = jax.random.randint(subkeys[2], (REGIONS, REGION_SLOTS, 1), -1, 4)
    cell_index = jnp.arange(CELLS, dtype=jnp.int32)
    across = 2 * (cell_index // SIDE) - SIDE + 1
    sideways = 2 * (cell_index % SIDE) - SIDE + 1
    on_side = tilt_rows * across + tilt_cols * sideways + offset * SIDE > 0
    speckle = jax.random.randint(subkeys[3], (REGIONS, REGION_SLOTS, CELLS), 0, 8) > 0
    return (on_side & speckle & occupied[..., None]).astype(jnp.int32)


def draw_pixels(key, part):
    key = jax.random.fold_in(key, 3)
    first_key, second_key = jax.random.split(key)
    full_shape = (REGIONS, REGION_SLOTS, SIDE, PATCH, SIDE, PATCH * 3)
    scale_shape = (REGIONS, REGION_SLOTS, SIDE, 1, SIDE, 1)
    values = jnp.clip(jax.random.normal(first_key, full_shape, jnp.float32), -4.0, 4.0)
    spread = jnp.exp(jax.random.uniform(second_key, scale_shape, jnp.float32, jnp.log(0.3), jnp.log(3.0)))
    return (values * spread).reshape(REGIONS, REGION_SLOTS, PX, PX * 3).astype(jnp.bfloat16)


def draw_dw_weight(key, part):
    key = jax.random.fold_in(key, 5)
    first_key, second_key = jax.random.split(key)
    values = jnp.clip(jax.random.normal(first_key, (KS * KS, C), jnp.float32), -4.0, 4.0)
    spread = jnp.exp(jax.random.uniform(second_key, (1, C), jnp.float32, jnp.log(0.3), jnp.log(3.0)))
    return values * spread / KS


def block_scale(rng, shape, pieces, low, high):
    gain, own = 1.0, jax.random.fold_in(rng, 6)
    for dim, blocks in pieces:
        draws = jnp.exp(jax.random.uniform(jax.random.fold_in(own, dim), (blocks,), jnp.float32, low / len(pieces), high / len(pieces)))
        gain = gain * jnp.repeat(draws, shape[dim] // blocks).reshape([-1 if axis == dim else 1 for axis in range(len(shape))])
    return gain


def centred(rng, dims, scale, limit, cuts=(), kind=jnp.bfloat16):
    loudness = block_scale(rng, dims, cuts, -0.22, 0.18) if cuts else 1.0
    drawn = jax.random.normal(rng, dims, jnp.float32) * scale * loudness
    return jnp.minimum(jnp.maximum(drawn, -limit), limit).astype(kind)


def setup_inputs(seed: int = 0) -> dict:
    key_list = jax.random.split(jax.random.key(seed), 12)
    return {
        "pixels": draw_pixels(jax.random.fold_in(key_list[11], 71), 0),
        "tissue": draw_tissue(jax.random.fold_in(key_list[11], 71), 0),
        "neighbours": draw_neighbours(jax.random.fold_in(key_list[11], 71), 0),
        "upstream": centred(key_list[3], (REGIONS, REGION_SLOTS, SIDE, SIDE * C), 1.0, 6.0, ((0, 4), (1, 32))),
        "stem_weight": centred(key_list[4], (PATCH * PATCH * 3, C), (PATCH * PATCH * 3) ** -0.5, 0.875),
        "stem_gain": jnp.clip(1.0 + 0.1 * jax.random.normal(key_list[5], (C,), jnp.float32), 0.5, 1.5),
        "dw_weight": draw_dw_weight(jax.random.fold_in(key_list[11], 71), 0),
        "norm_gain": jnp.clip(1.0 + 0.1 * jax.random.normal(key_list[7], (C,), jnp.float32), 0.5, 1.5),
        "up_weight": centred(key_list[8], (C, HID), C ** -0.5, 0.625),
        "down_weight": centred(key_list[9], (HID, C), HID ** -0.5, 0.3125),
        "layer_scale": jnp.clip(jnp.exp(jax.random.uniform(key_list[10], (C,), jnp.float32, math.log(0.2), math.log(1.0))), 0.2, 1.0),
    }


eps = 1e-06

def normalize(values):
    mean = lax.optimization_barrier(jnp.mean(values, axis=-1, keepdims=True))
    centered = values - mean
    inverse = lax.rsqrt(lax.optimization_barrier(jnp.mean(centered * centered, axis=-1, keepdims=True)) + eps)
    return (centered * inverse, inverse)

def patchify(one_tile):
    return one_tile.reshape(SIDE, PATCH, SIDE, PATCH * 3).transpose(0, 2, 1, 3).reshape(SIDE, SIDE, PATCH * PATCH * 3)

def stem_cells(patches, stem_weight, stem_gain):
    flat = patches.reshape(-1, patches.shape[-1])
    raw_out = jnp.dot(flat, stem_weight, preferred_element_type=jnp.float32)
    normed, inverse = normalize(raw_out)
    return (normed * stem_gain).astype(jnp.bfloat16).reshape(patches.shape[:-1] + (stem_weight.shape[1],))

def gelu_parts(hidden):
    normal_cdf = 0.5 * (1.0 + lax.erf(hidden * 0.7071067811865476))
    density = jnp.exp(-0.5 * hidden * hidden) * 0.3989422804014327
    return (hidden * normal_cdf, normal_cdf + hidden * density)

def assemble(center, neighbour_cells):
    inner = SIDE - RIM
    upper_band = jnp.concatenate([neighbour_cells[4][inner:, inner:], neighbour_cells[0][inner:], neighbour_cells[5][inner:, :RIM]], axis=1)
    middle = jnp.concatenate([neighbour_cells[2][:, inner:], center, neighbour_cells[3][:, :RIM]], axis=1)
    lower_band = jnp.concatenate([neighbour_cells[6][:RIM, inner:], neighbour_cells[1][:RIM], neighbour_cells[7][:RIM, :RIM]], axis=1)
    return jnp.concatenate([upper_band, middle, lower_band], axis=0)

def block_step(padded, tissue_cells, upstream_tile, dw_weight, norm_gain, up_weight, down_weight, layer_scale, loss_factor):
    channels = dw_weight.shape[1]
    side = upstream_tile.shape[0]
    width = side * channels
    count = side * side
    mixed_sum = jnp.zeros((side, width), jnp.float32)
    for kernel_tap in range(KS * KS):
        row_at = kernel_tap // KS
        col_at = kernel_tap % KS
        window = padded[row_at:row_at + side, col_at * channels:col_at * channels + width].astype(jnp.float32)
        mixed_sum = mixed_sum + window * jnp.tile(dw_weight[kernel_tap], side)
    center = padded[RIM:RIM + side, RIM * channels:RIM * channels + width]
    normed, inverse = normalize(mixed_sum.reshape(count, channels))
    lowered = (normed * norm_gain).astype(jnp.bfloat16)
    hidden = jnp.dot(lowered, up_weight, preferred_element_type=jnp.float32)
    active, steepness = gelu_parts(hidden)
    active = active.astype(jnp.bfloat16)
    branch = jnp.dot(active, down_weight, preferred_element_type=jnp.float32)
    tissue_weight = tissue_cells.astype(jnp.float32)[:, None]
    summed = center.reshape(count, channels).astype(jnp.float32) + layer_scale * branch
    features = (summed * tissue_weight).astype(jnp.bfloat16).reshape(side, width)
    grad_out = upstream_tile.reshape(count, channels).astype(jnp.float32) * tissue_weight * loss_factor
    grad_scale = lax.optimization_barrier(jnp.sum(grad_out * branch, axis=0))
    grad_branch = (grad_out * layer_scale).astype(jnp.bfloat16)
    grad_down = jnp.dot(active.T, grad_branch, preferred_element_type=jnp.float32)
    grad_active = jnp.dot(grad_branch, down_weight.T, preferred_element_type=jnp.float32)
    grad_hidden = (grad_active * steepness).astype(jnp.bfloat16)
    grad_up = jnp.dot(lowered.T, grad_hidden, preferred_element_type=jnp.float32)
    grad_lowered = jnp.dot(grad_hidden, up_weight.T, preferred_element_type=jnp.float32)
    grad_gain = lax.optimization_barrier(jnp.sum(grad_lowered * normed, axis=0))
    scaled = grad_lowered * norm_gain
    grad_mixed = inverse * (scaled - lax.optimization_barrier(jnp.mean(scaled, axis=-1, keepdims=True)) - normed * lax.optimization_barrier(jnp.mean(scaled * normed, axis=-1, keepdims=True)))
    grad_mixed = grad_mixed.reshape(side, width)
    tap_terms = []
    for kernel_tap in range(KS * KS):
        row_at = kernel_tap // KS
        col_at = kernel_tap % KS
        window = padded[row_at:row_at + side, col_at * channels:col_at * channels + width].astype(jnp.float32)
        tap_terms.append(lax.optimization_barrier(jnp.sum(lax.optimization_barrier(jnp.sum(window * grad_mixed, axis=0)).reshape(side, channels), axis=0)))
    grad_dw = jnp.stack(tap_terms, axis=0)
    return (features, (grad_dw, grad_gain, grad_up, grad_down, grad_scale))

def reference(pixels, tissue, neighbours, upstream, stem_weight, stem_gain, dw_weight, norm_gain, up_weight, down_weight, layer_scale):
    regions = pixels.shape[0]
    region_slots = pixels.shape[1]
    flat_pixels = pixels.reshape(regions * region_slots, PX, PX * 3)
    all_cells = lax.map(lambda one_tile: stem_cells(patchify(one_tile), stem_weight, stem_gain), flat_pixels)
    all_cells = all_cells.reshape(regions, region_slots, SIDE, SIDE, C)
    loss_factor = (N_SLAB * N_TILE * SLOTS * CELLS) ** (-0.5)

    def visit_slot(totals, position):
        region = position // region_slots
        slot_index = position - region * region_slots
        region_cells = all_cells[region]
        adjacent = neighbours[region, slot_index]
        neighbour_cells = jnp.take(region_cells, jnp.maximum(adjacent, 0), axis=0)
        neighbour_cells = jnp.where((adjacent >= 0)[:, None, None, None], neighbour_cells, jnp.zeros_like(neighbour_cells))
        padded = assemble(region_cells[slot_index], neighbour_cells)
        padded = padded.reshape(SIDE + 2 * RIM, (SIDE + 2 * RIM) * C)
        features, grad_terms = block_step(padded, tissue[region, slot_index], upstream[region, slot_index], dw_weight, norm_gain, up_weight, down_weight, layer_scale, loss_factor)
        updated = tuple((left_term + right_term for left_term, right_term in zip(totals, grad_terms)))
        return (updated, features)
    initial = (jnp.zeros((KS * KS, C), jnp.float32), jnp.zeros((C,), jnp.float32), jnp.zeros((C, HID), jnp.float32), jnp.zeros((HID, C), jnp.float32), jnp.zeros((C,), jnp.float32))
    totals, features = lax.scan(visit_slot, initial, jnp.arange(regions * region_slots, dtype=jnp.int32))
    features = features.reshape(regions, region_slots, SIDE, SIDE * C)
    return (features, totals[0], totals[1], totals[2], totals[3], totals[4])
```

```python
import functools

import jax
import jax.numpy as jnp
from jax import lax
from jax.experimental import pallas as pl
from jax.experimental.pallas import tpu as pltpu
from jax.sharding import PartitionSpec as P

MESH = pl.DeviceIdType.MESH
C = 96
HID = 384
PATCH = 4
KS = 7
SIDE = 32
RIM = 3
REACH = 5
SLOTS = 4
LANES = SLOTS * SIDE
PADW = SIDE + 2 * RIM
GROUP = 16
GROUPS = C // GROUP
BLOCK = 8
BLOCKS = SIDE // BLOCK
TAPW = (BLOCK + RIM * 2) * GROUP
BAND = KS * TAPW
EPS = 1e-06
CHUNKS = 16
MAIN = 48
CHUNK_ROWS = MAIN + 8

BF16 = jnp.bfloat16
F32 = jnp.float32


def iota(shape, dim):
    return lax.broadcasted_iota(jnp.int32, shape, dim)


def onehot(mask):
    return jnp.where(mask, 1.0, 0.0).astype(BF16)


def mm(a, b):
    return lax.dot_general(a, b, (((1,), (0,)), ((), ())), preferred_element_type=F32)


def mm_nt(a, b):
    return lax.dot_general(a, b, (((1,), (1,)), ((), ())), preferred_element_type=F32)


def column(row, lanes):
    return jnp.transpose(jnp.broadcast_to(row, (lanes, row.shape[1])))


def stem_kernel(tiles, pix_ref, w_ref, gain_ref, ct_ref, recv_ref, strip_ref, send_sem, recv_sem):
    me = lax.axis_index("tile")
    barrier = pltpu.get_barrier_semaphore()
    for d in range(1, REACH + 1):
        for sign in (-1, 1):
            peer = lax.rem(me + sign * d + tiles, tiles)
            pl.semaphore_signal(barrier, inc=1, device_id={"tile": peer}, device_id_type=MESH)

    pix = pix_ref[...].reshape(SLOTS * SIDE * PATCH, SIDE * PATCH * 3)
    rows = SLOTS * SIDE * PATCH
    k_at, n_at = iota((rows, rows), 0), iota((rows, rows), 1)
    pick = onehot(k_at == PATCH * (n_at % LANES) + n_at // LANES)
    pix_t = mm(jnp.transpose(pix), pick).astype(BF16)

    q = PATCH * 3
    wt = jnp.transpose(w_ref[...])
    k_at, n_at = iota((PATCH * q, PATCH * 4 * q), 0), iota((PATCH * q, PATCH * 4 * q), 1)
    spread = onehot((k_at // q == n_at // (4 * q)) & (k_at % q == n_at % q))
    wide = mm(wt, spread)
    wide = jnp.concatenate([wide] * 4, axis=0)
    r_at, n_at = iota(wide.shape, 0), iota(wide.shape, 1)
    block_w = jnp.where(r_at // C == (n_at % (4 * q)) // q, wide, 0.0).astype(BF16)

    gain = column(gain_ref[...], LANES)
    eight = SIDE // 4
    operand = jnp.concatenate(
        [
            jnp.concatenate(
                [pix_t[4 * q * g : 4 * q * (g + 1), LANES * pr : LANES * (pr + 1)] for pr in range(PATCH)],
                axis=0,
            )
            for g in range(eight)
        ],
        axis=1,
    )
    raw = mm(block_w, operand)
    for v in range(4):
        part = raw[C * v : C * (v + 1)]
        mean = jnp.sum(part, axis=0, keepdims=True) * (1.0 / C)
        part = part - mean
        inverse = lax.rsqrt(jnp.sum(part * part, axis=0, keepdims=True) * (1.0 / C) + EPS)
        part = part * inverse
        for g in range(eight):
            ct_ref[4 * g + v] = (part[:, LANES * g : LANES * (g + 1)] * gain).astype(BF16)

    k_at, n_at = iota((LANES, 6 * LANES), 0), iota((LANES, 6 * LANES), 1)
    kind = n_at // LANES
    row_at = jnp.where(kind < RIM, kind, SIDE - 2 * RIM + kind)
    base = onehot((k_at // SIDE == n_at % SLOTS) & (k_at % SIDE == row_at))
    col_of = (n_at % LANES) // SLOTS
    packed = jnp.zeros((C, 6 * LANES), F32)
    for w in range(0, SIDE, 8):
        left = jnp.concatenate([ct_ref[w + i] for i in range(8)], axis=1)
        right = jnp.concatenate(
            [jnp.where(col_of == w + i, base, jnp.zeros_like(base)) for i in range(8)], axis=0
        )
        packed = packed + mm(left, right)
    for i in range(6):
        strip_ref[i] = packed[:, LANES * i : LANES * (i + 1)].astype(BF16)

    pl.semaphore_wait(barrier, 2 * REACH)
    copies = []
    for d in range(1, REACH + 1):
        back = lax.rem(me - d + tiles, tiles)
        ahead = lax.rem(me + d, tiles)
        if d == 1:
            copies.append((strip_ref.at[pl.ds(0, RIM)], 10, back))
            copies.append((strip_ref.at[pl.ds(RIM, RIM)], 11, ahead))
        copies.append((ct_ref.at[pl.ds(0, RIM)], d - 1, back))
        copies.append((ct_ref.at[pl.ds(SIDE - RIM, RIM)], REACH + d - 1, ahead))
    started = []
    for source, at, peer in copies:
        copy = pltpu.make_async_remote_copy(
            src_ref=source,
            dst_ref=recv_ref.at[at],
            send_sem=send_sem.at[at],
            recv_sem=recv_sem.at[at],
            device_id={"tile": peer},
            device_id_type=MESH,
        )
        copy.start()
        started.append(copy)
    for copy in started:
        copy.wait()


def gelu_parts(hidden):
    normal_cdf = 0.5 * (1.0 + lax.erf(hidden * 0.7071067811865476))
    density = jnp.exp(-0.5 * hidden * hidden) * 0.3989422804014327
    return (hidden * normal_cdf, normal_cdf + hidden * density)


def block_kernel(
    loss_factor,
    nb_ref,
    ct_ref,
    recv_ref,
    up_stream_ref,
    tissue_ref,
    dw_ref,
    gain_ref,
    scale_ref,
    up_ref,
    down_ref,
    feat_ref,
    sums_ref,
    pt_ref,
    ht_ref,
    side_ref,
    mixed_ref,
    gm_ref,
    ut_ref,
    ft_ref,
    gd_ref,
    gu_ref,
    gg_ref,
    gs_ref,
):
    me = lax.axis_index("tile")
    lane = iota((1, LANES), 1)
    slot_of, row_of = lane // SIDE, lane % SIDE

    def per_tile(direction, rule):
        out = []
        for t in range(SLOTS):
            n = nb_ref[t, direction]
            out.append(jnp.where(n >= 0, rule(jnp.maximum(n, 0)), -1))
        return out

    def spread(values, shift):
        result = jnp.full((1, LANES), -1, jnp.int32)
        for t in range(SLOTS):
            result = jnp.where(slot_of == (t + shift) % SLOTS, values[t], result)
        return result

    def add_row(index, row):
        return jnp.where(index >= 0, index + row, -1)

    top = row_of >= SIDE - RIM
    bottom = row_of < RIM

    for east in (0, 1):
        def rule(n, east=east):
            away = n // SLOTS - me
            away = away if east else -away
            return away * LANES + (n % SLOTS) * SIDE

        straight = spread(per_tile(2 + east, rule), 0)
        above = spread(per_tile(4 + east, rule), -1)
        below = spread(per_tile(6 + east, rule), 1)
        halo = jnp.where(top, above, jnp.where(bottom, below, -1))
        index = jnp.concatenate([add_row(straight, row_of), add_row(halo, row_of)], axis=1)
        select = onehot(iota(((REACH + 1) * LANES, 2 * LANES), 0) == index)
        first = 0 if east else SIDE - RIM
        base = 0 if east else REACH
        for i in range(RIM):
            source = jnp.concatenate(
                [ct_ref[first + i]] + [recv_ref[base + d, i] for d in range(REACH)], axis=1
            )
            side_ref[east * RIM + i] = mm(source, select).astype(BF16)

    def own_rule(n):
        return jnp.where(n // SLOTS == me, (n % SLOTS) * SIDE, -1)

    def other_rule(n):
        return jnp.where(n // SLOTS == me, -1, n % SLOTS)

    own_above = spread(per_tile(0, own_rule), -1)
    own_below = spread(per_tile(1, own_rule), 1)
    own = add_row(jnp.where(top, own_above, jnp.where(bottom, own_below, -1)), row_of)
    select_own = onehot(iota((LANES, LANES), 0) == own)
    far_above = spread(per_tile(0, other_rule), -1)
    far_below = spread(per_tile(1, other_rule), 1)
    far = jnp.where(
        top,
        jnp.where(far_above >= 0, (row_of - (SIDE - RIM)) * SLOTS + far_above, -1),
        jnp.where(bottom & (far_below >= 0), (RIM + row_of) * SLOTS + far_below, -1),
    )
    k_at = iota((2 * RIM * LANES, LANES), 0)
    far_base = onehot((k_at // LANES) * SLOTS + k_at % SLOTS == far)
    col_of = (k_at % LANES) // SLOTS
    strips = jnp.concatenate(
        [recv_ref[11, i] for i in range(RIM)] + [recv_ref[10, i] for i in range(RIM)], axis=1
    )
    for w in range(0, SIDE, 4):
        select_far = jnp.concatenate(
            [jnp.where(col_of == w + i, far_base, jnp.zeros_like(far_base)) for i in range(4)], axis=1
        )
        got = mm(strips, select_far)
        for i in range(4):
            near = mm(ct_ref[w + i], select_own)
            ht_ref[w + i] = (near + got[:, LANES * i : LANES * (i + 1)]).astype(BF16)

    def fill(at, centre, halo):
        for a in range(KS):
            s = a - RIM
            if s > 0:
                value = pltpu.roll(jnp.where(row_of < s, halo, centre), LANES - s, 1)
            elif s < 0:
                value = pltpu.roll(jnp.where(row_of >= SIDE + s, halo, centre), -s, 1)
            else:
                value = centre
            pt_ref[a, at] = value

    for i in range(RIM):
        for east in (0, 1):
            sides = side_ref[east * RIM + i]
            fill(east * (RIM + SIDE) + i, sides[:, :LANES], sides[:, LANES:])

    def fill_step(w, carry):
        fill(RIM + w, ct_ref[w], ht_ref[w])
        return carry

    lax.fori_loop(0, SIDE, fill_step, 0)

    for w in range(0, SIDE, 4):
        part = jnp.transpose(up_stream_ref[:, C * w : C * (w + 4)])
        for i in range(4):
            ut_ref[w + i] = part[C * i : C * (i + 1)]

    def window(g):
        return jnp.concatenate(
            [
                jnp.concatenate(
                    [
                        pt_ref[a, BLOCK * j : BLOCK * j + TAPW // GROUP, GROUP * g : GROUP * (g + 1)].reshape(
                            TAPW, LANES
                        )
                        for a in range(KS)
                    ],
                    axis=0,
                )
                for j in range(BLOCKS)
            ],
            axis=1,
        )

    r_at, n_at = iota((GROUP, BAND), 0), iota((GROUP, BAND), 1)
    diagonal = r_at == n_at % GROUP
    for g in range(GROUPS):
        first = jnp.where(diagonal, dw_ref[pl.ds(g, 1), :], 0.0)
        band = jnp.concatenate(
            [first] + [pltpu.roll(first, GROUP * w, 1) for w in range(1, BLOCK)], axis=0
        ).astype(BF16)
        out = mm(band, window(g))
        for w in range(BLOCK):
            mixed_ref[w, GROUP * g : GROUP * (g + 1), :] = out[GROUP * w : GROUP * (w + 1)]

    gain = column(gain_ref[...], LANES)
    scale = column(scale_ref[...], LANES)
    gain = jnp.concatenate([gain] * BLOCKS, axis=1)
    scale = jnp.concatenate([scale] * BLOCKS, axis=1)
    up_w = up_ref[...]
    down_w = down_ref[...]
    up_t = jnp.transpose(up_w)
    down_t = jnp.transpose(down_w)
    gd_ref[...] = jnp.zeros_like(gd_ref)
    gu_ref[...] = jnp.zeros_like(gu_ref)
    gg_ref[...] = jnp.zeros_like(gg_ref)
    gs_ref[...] = jnp.zeros_like(gs_ref)

    def gather(ref, w, offset=0):
        return jnp.concatenate([ref[offset + BLOCK * j + w] for j in range(BLOCKS)], axis=1)

    def fold(values):
        total = values[:, :LANES]
        for j in range(1, BLOCKS):
            total = total + values[:, LANES * j : LANES * (j + 1)]
        return total

    def step(w, carry):
        mixed = mixed_ref[w]
        mean = jnp.sum(mixed, axis=0, keepdims=True) * (1.0 / C)
        centered = mixed - mean
        inverse = lax.rsqrt(jnp.sum(centered * centered, axis=0, keepdims=True) * (1.0 / C) + EPS)
        normed = centered * inverse
        lowered = (normed * gain).astype(BF16)
        hidden = mm(up_t, lowered)
        active, steepness = gelu_parts(hidden)
        active = active.astype(BF16)
        branch = mm(down_t, active)
        tissue = gather(tissue_ref, w)
        summed = gather(ct_ref, w).astype(F32) + scale * branch
        features = (summed * tissue).astype(BF16)
        grad_out = gather(ut_ref, w).astype(F32) * (tissue * loss_factor)
        gs_ref[...] += fold(grad_out * branch)
        grad_branch = (grad_out * scale).astype(BF16)
        gd_ref[...] += mm_nt(active, grad_branch)
        grad_active = mm(down_w, grad_branch)
        grad_hidden = (grad_active * steepness).astype(BF16)
        gu_ref[...] += mm_nt(grad_hidden, lowered)
        grad_lowered = mm(up_w, grad_hidden)
        gg_ref[...] += fold(grad_lowered * normed)
        scaled = grad_lowered * gain
        mean_one = jnp.sum(scaled, axis=0, keepdims=True) * (1.0 / C)
        mean_two = jnp.sum(scaled * normed, axis=0, keepdims=True) * (1.0 / C)
        gm_ref[w] = (inverse * (scaled - mean_one - normed * mean_two)).astype(BF16)
        for j in range(BLOCKS):
            ft_ref[BLOCK * j + w] = features[:, LANES * j : LANES * (j + 1)]
        return carry

    lax.fori_loop(0, BLOCK, step, 0)

    for w in range(0, SIDE, 4):
        part = jnp.concatenate([ft_ref[w + i] for i in range(4)], axis=0)
        feat_ref[:, C * w : C * (w + 4)] = jnp.transpose(part)

    low = []
    for g in range(GROUPS):
        left = jnp.concatenate([gm_ref[w, GROUP * g : GROUP * (g + 1), :] for w in range(BLOCK)], axis=0)
        full = mm_nt(left, window(g))
        total = None
        for w in range(BLOCK):
            part = jnp.where(diagonal, full[GROUP * w : GROUP * (w + 1)], 0.0)
            part = part[:8] + part[8:]
            if w:
                part = pltpu.roll(part, BAND - GROUP * w, 1)
            total = part if total is None else total + part
        total = jnp.sum(total, axis=0, keepdims=True)
        low.append(
            jnp.concatenate([total[:, TAPW * a : TAPW * a + KS * GROUP] for a in range(KS)], axis=1)
        )
    width = CHUNKS * 128
    filler = jnp.zeros((1, width - KS * KS * GROUP), F32)
    low = [jnp.concatenate([row, filler], axis=1) for row in low]
    for ref in (gg_ref, gs_ref):
        row = jnp.sum(jnp.transpose(ref[...]), axis=0, keepdims=True)
        low.append(jnp.concatenate([row, jnp.zeros((1, width - C), F32)], axis=1))
    low = jnp.concatenate(low, axis=0)
    padding = jnp.zeros((MAIN, 128 - C), F32)
    for i in range(CHUNKS):
        ref, at = (gd_ref, i) if i < 8 else (gu_ref, i - 8)
        rows = ref[MAIN * at : MAIN * (at + 1), :]
        sums_ref[i, :MAIN, :] = jnp.concatenate([rows, padding], axis=1)
        sums_ref[i, MAIN:, :] = low[:, 128 * i : 128 * (i + 1)]


def reduce_kernel(x_ref, gd_ref, gu_ref, low_ref, first, second, part, res, s1, r1, s2, r2, s3, r3):
    tile = lax.axis_index("tile")
    slab = lax.axis_index("slab")
    me_a = tile % 4 + 4 * slab
    me_b = tile // 4

    def peer_a(k):
        i = lax.rem(me_a + k, CHUNKS)
        return i, {"tile": me_b * 4 + i % 4, "slab": i // 4}

    def peer_b(k):
        j = lax.rem(me_b + k, 8)
        return j, {"tile": j * 4 + tile % 4, "slab": slab}

    barrier = pltpu.get_barrier_semaphore()
    for k in range(1, CHUNKS):
        pl.semaphore_signal(barrier, inc=1, device_id=peer_a(k)[1], device_id_type=MESH)
    for k in range(1, 8):
        pl.semaphore_signal(barrier, inc=1, device_id=peer_b(k)[1], device_id_type=MESH)
    pl.semaphore_wait(barrier, CHUNKS - 1 + 7)

    def send(source, target, send_sem, recv_sem, device):
        copy = pltpu.make_async_remote_copy(
            src_ref=source,
            dst_ref=target,
            send_sem=send_sem,
            recv_sem=recv_sem,
            device_id=device,
            device_id_type=MESH,
        )
        copy.start()
        return copy

    copies = []
    for k in range(1, CHUNKS):
        i, device = peer_a(k)
        copies.append(send(x_ref.at[i], first.at[k], s1.at[k], r1.at[k], device))
    total = x_ref[me_a]
    for k in range(1, CHUNKS):
        copies[k - 1].wait_recv()
        total = total + first[k]
    part[...] = total
    second[me_b] = total
    again = []
    for k in range(1, 8):
        j, device = peer_b(k)
        again.append(send(part, second.at[me_b], s2.at[k], r2.at[k], device))
    for copy in again:
        copy.wait_recv()
    total = second[0]
    for k in range(1, 8):
        total = total + second[k]
    res[me_a] = total
    last = []
    for k in range(1, CHUNKS):
        i, device = peer_a(k)
        last.append(send(res.at[me_a], res.at[me_a], s3.at[k], r3.at[k], device))
    for copy in last:
        copy.wait_recv()
    for i in range(8):
        gd_ref[MAIN * i : MAIN * (i + 1), :] = res[i, :MAIN, :C]
    whole = jnp.concatenate([res[8 + i, :MAIN, :] for i in range(8)], axis=0)
    gu_ref[...] = jnp.transpose(whole)[:C, :]
    low_ref[...] = jnp.concatenate([res[i, MAIN:, :] for i in range(7)], axis=1)
    for copy in copies + again + last:
        copy.wait_send()


def vmem(count):
    return [pl.BlockSpec(memory_space=pltpu.VMEM)] * count


def local(
    pixels,
    tissue,
    neighbours,
    upstream,
    stem_weight,
    stem_gain,
    dw_weight,
    norm_gain,
    up_weight,
    down_weight,
    layer_scale,
):
    tiles = lax.axis_size("tile")
    loss_factor = (tiles * lax.axis_size("slab") * SLOTS * SIDE * SIDE) ** (-0.5)
    cells, received = pl.pallas_call(
        functools.partial(stem_kernel, tiles),
        out_shape=(
            jax.ShapeDtypeStruct((SIDE, C, LANES), BF16),
            jax.ShapeDtypeStruct((2 * REACH + 2, RIM, C, LANES), BF16),
        ),
        in_specs=vmem(3),
        out_specs=tuple(vmem(2)),
        scratch_shapes=[
            pltpu.VMEM((2 * RIM, C, LANES), BF16),
            pltpu.SemaphoreType.DMA((2 * REACH + 2,)),
            pltpu.SemaphoreType.DMA((2 * REACH + 2,)),
        ],
        compiler_params=pltpu.CompilerParams(
            collective_id=0, has_side_effects=True, vmem_limit_bytes=48 * 1024 * 1024
        ),
        name="stem_exchange",
    )(pixels[0], stem_weight, stem_gain[None])

    taps = dw_weight.reshape(KS, KS, GROUPS, GROUP).transpose(2, 0, 1, 3)
    taps = jnp.pad(taps, ((0, 0), (0, 0), (0, TAPW // GROUP - KS), (0, 0))).reshape(GROUPS, BAND)
    tissue_t = tissue[0].reshape(LANES, SIDE).T.astype(F32).reshape(SIDE, 1, LANES)
    features, sums = pl.pallas_call(
        functools.partial(block_kernel, loss_factor),
        out_shape=(
            jax.ShapeDtypeStruct((LANES, SIDE * C), BF16),
            jax.ShapeDtypeStruct((CHUNKS, CHUNK_ROWS, 128), F32),
        ),
        in_specs=[pl.BlockSpec(memory_space=pltpu.SMEM)] + vmem(9),
        out_specs=tuple(vmem(2)),
        scratch_shapes=[
            pltpu.VMEM((KS, PADW, C, LANES), BF16),
            pltpu.VMEM((SIDE, C, LANES), BF16),
            pltpu.VMEM((2 * RIM, C, 2 * LANES), BF16),
            pltpu.VMEM((BLOCK, C, BLOCKS * LANES), F32),
            pltpu.VMEM((BLOCK, C, BLOCKS * LANES), BF16),
            pltpu.VMEM((SIDE, C, LANES), BF16),
            pltpu.VMEM((SIDE, C, LANES), BF16),
            pltpu.VMEM((HID, C), F32),
            pltpu.VMEM((HID, C), F32),
            pltpu.VMEM((C, LANES), F32),
            pltpu.VMEM((C, LANES), F32),
        ],
        compiler_params=pltpu.CompilerParams(vmem_limit_bytes=56 * 1024 * 1024),
        name="block",
    )(
        neighbours[0],
        cells,
        received,
        upstream.reshape(LANES, SIDE * C),
        tissue_t,
        taps,
        norm_gain[None],
        layer_scale[None],
        up_weight,
        down_weight,
    )

    dma = pltpu.SemaphoreType.DMA
    grad_down, grad_up, low = pl.pallas_call(
        reduce_kernel,
        out_shape=(
            jax.ShapeDtypeStruct((HID, C), F32),
            jax.ShapeDtypeStruct((C, HID), F32),
            jax.ShapeDtypeStruct((8, 7 * 128), F32),
        ),
        in_specs=vmem(1),
        out_specs=tuple(vmem(3)),
        scratch_shapes=[
            pltpu.VMEM((CHUNKS, CHUNK_ROWS, 128), F32),
            pltpu.VMEM((8, CHUNK_ROWS, 128), F32),
            pltpu.VMEM((CHUNK_ROWS, 128), F32),
            pltpu.VMEM((CHUNKS, CHUNK_ROWS, 128), F32),
            dma((CHUNKS,)),
            dma((CHUNKS,)),
            dma((8,)),
            dma((8,)),
            dma((CHUNKS,)),
            dma((CHUNKS,)),
        ],
        compiler_params=pltpu.CompilerParams(
            collective_id=1, has_side_effects=True, vmem_limit_bytes=48 * 1024 * 1024
        ),
        name="sum_gradients",
    )(sums)
    grad_dw = low[:GROUPS, : KS * KS * GROUP].reshape(GROUPS, KS * KS, GROUP).transpose(1, 0, 2)
    grad_dw = grad_dw.reshape(KS * KS, C)
    return (
        features.reshape(upstream.shape),
        grad_dw,
        low[GROUPS, :C],
        grad_up,
        grad_down,
        low[GROUPS + 1, :C],
    )


def solution(mesh):
    placed = (
        P("slab", "tile", None, None),
        P("slab", "tile", None),
        P("slab", "tile", None),
        P("slab", "tile", None, None),
        P(),
        P(),
        P(),
        P(),
        P(),
        P(),
        P(),
    )
    return jax.shard_map(
        local,
        mesh=mesh,
        in_specs=placed,
        out_specs=(P("slab", "tile", None, None), P(), P(), P(), P(), P()),
        check_vma=False,
    )
```

```python
import functools

import jax
import jax.numpy as jnp
from jax import lax
from jax.experimental import pallas as pl
from jax.experimental.pallas import tpu as pltpu
from jax.sharding import PartitionSpec as P

MESH = pl.DeviceIdType.MESH
C = 96
HID = 384
PATCH = 4
KS = 7
SIDE = 32
RIM = 3
REACH = 5
SLOTS = 4
LANES = SLOTS * SIDE
PADW = SIDE + 2 * RIM
GROUP = 16
GROUPS = C // GROUP
BLOCK = 8
BLOCKS = SIDE // BLOCK
TAPW = (BLOCK + RIM * 2) * GROUP
BAND = KS * TAPW
EPS = 1e-06
FILL_UNROLL = 32
STEP_UNROLL = 2
PLANE = 16
PIECE = HID // PLANE
PIECE_PAD = 32

BF16 = jnp.bfloat16
F32 = jnp.float32


def iota(shape, dim):
    return lax.broadcasted_iota(jnp.int32, shape, dim)


def onehot(mask):
    return jnp.where(mask, 1.0, 0.0).astype(BF16)


def mm(a, b):
    return lax.dot_general(a, b, (((1,), (0,)), ((), ())), preferred_element_type=F32)


def mm_nt(a, b):
    return lax.dot_general(a, b, (((1,), (1,)), ((), ())), preferred_element_type=F32)


def column(row, lanes):
    return jnp.transpose(jnp.broadcast_to(row, (lanes, row.shape[1])))


def gelu_parts(hidden):
    normal_cdf = 0.5 * (1.0 + lax.erf(hidden * 0.7071067811865476))
    density = jnp.exp(-0.5 * hidden * hidden) * 0.3989422804014327
    return (hidden * normal_cdf, normal_cdf + hidden * density)


def remote(source, target, send_sem, recv_sem, device):
    return pltpu.make_async_remote_copy(
        src_ref=source,
        dst_ref=target,
        send_sem=send_sem,
        recv_sem=recv_sem,
        device_id=device,
        device_id_type=MESH,
    )


def whole_kernel(
    tiles,
    loss_factor,
    nb_ref,
    pix_ref,
    stem_ref,
    stem_gain_ref,
    up_stream_ref,
    tissue_ref,
    dw_ref,
    gain_ref,
    up_ref,
    down_t_ref,
    scale_ref,
    feat_ref,
    out_dw_ref,
    out_gain_ref,
    out_up_ref,
    out_down_ref,
    out_scale_ref,
    ct_ref,
    strip_ref,
    recv_ref,
    pt_ref,
    ht_ref,
    side_ref,
    band_ref,
    mixed_ref,
    gm_ref,
    ut_ref,
    ft_ref,
    ts_ref,
    acc_ref,
    gg_ref,
    gs_ref,
    big_ref,
    core_in,
    rs_src,
    rs_in,
    y_buf,
    ag_buf,
    small_core,
    small_plane,
    small_y,
    send_sem,
    recv_sem,
    sum_send,
    sum_recv,
):
    me = lax.axis_index("tile")
    slab = lax.axis_index("slab")
    core = slab % 2
    y_hi = slab // 2
    me_plane = me % PLANE
    y_lo = me // PLANE
    me_y = y_lo + 2 * y_hi

    partner = {"tile": me, "slab": 2 * y_hi + (1 - core)}

    def plane_peer(k):
        i = lax.rem(me_plane + k, PLANE)
        return i, {"tile": y_lo * PLANE + i, "slab": slab}

    def y_peer(k):
        other_lo = lax.rem(y_lo + k % 2, 2)
        other_hi = lax.rem(y_hi + k // 2, 2)
        return {"tile": other_lo * PLANE + me_plane, "slab": 2 * other_hi + core}

    barrier = pltpu.get_barrier_semaphore()
    greeted = [
        {"tile": lax.rem(me + sign * d + tiles, tiles)} for d in range(1, REACH + 1) for sign in (-1, 1)
    ]
    greeted += [partner]
    greeted += [plane_peer(k)[1] for k in range(1, PLANE)]
    greeted += [y_peer(k) for k in range(1, 4)]
    for device in greeted:
        pl.semaphore_signal(barrier, inc=1, device_id=device, device_id_type=MESH)

    pix = pix_ref[...].reshape(SLOTS * SIDE * PATCH, SIDE * PATCH * 3)
    rows = SLOTS * SIDE * PATCH
    k_at, n_at = iota((rows, rows), 0), iota((rows, rows), 1)
    pick = onehot(k_at == PATCH * (n_at % LANES) + n_at // LANES)
    pix_t = mm(jnp.transpose(pix), pick).astype(BF16)

    q = PATCH * 3
    wt = jnp.transpose(stem_ref[...])
    k_at, n_at = iota((PATCH * q, PATCH * 4 * q), 0), iota((PATCH * q, PATCH * 4 * q), 1)
    spread_q = onehot((k_at // q == n_at // (4 * q)) & (k_at % q == n_at % q))
    wide = mm(wt, spread_q)
    wide = jnp.concatenate([wide] * 4, axis=0)
    r_at, n_at = iota(wide.shape, 0), iota(wide.shape, 1)
    block_w = jnp.where(r_at // C == (n_at % (4 * q)) // q, wide, 0.0).astype(BF16)

    stem_gain = column(stem_gain_ref[...], LANES)
    eight = SIDE // 4
    operand = jnp.concatenate(
        [
            jnp.concatenate(
                [pix_t[4 * q * g : 4 * q * (g + 1), LANES * pr : LANES * (pr + 1)] for pr in range(PATCH)],
                axis=0,
            )
            for g in range(eight)
        ],
        axis=1,
    )
    raw = mm(block_w, operand)
    for v in range(4):
        part = raw[C * v : C * (v + 1)]
        mean = jnp.sum(part, axis=0, keepdims=True) * (1.0 / C)
        part = part - mean
        inverse = lax.rsqrt(jnp.sum(part * part, axis=0, keepdims=True) * (1.0 / C) + EPS)
        part = part * inverse
        for g in range(eight):
            ct_ref[4 * g + v] = (part[:, LANES * g : LANES * (g + 1)] * stem_gain).astype(BF16)

    k_at, n_at = iota((LANES, 6 * LANES), 0), iota((LANES, 6 * LANES), 1)
    kind = n_at // LANES
    row_at = jnp.where(kind < RIM, kind, SIDE - 2 * RIM + kind)
    base = onehot((k_at // SIDE == n_at % SLOTS) & (k_at % SIDE == row_at))
    col_of = (n_at % LANES) // SLOTS
    packed = jnp.zeros((C, 6 * LANES), F32)
    for w in range(0, SIDE, 8):
        left = jnp.concatenate([ct_ref[w + i] for i in range(8)], axis=1)
        right = jnp.concatenate(
            [jnp.where(col_of == w + i, base, jnp.zeros_like(base)) for i in range(8)], axis=0
        )
        packed = packed + mm(left, right)
    for i in range(6):
        strip_ref[i] = packed[:, LANES * i : LANES * (i + 1)].astype(BF16)

    pl.semaphore_wait(barrier, len(greeted))
    strips_sent, sides_sent = [], []
    for d in range(1, REACH + 1):
        back = lax.rem(me - d + tiles, tiles)
        ahead = lax.rem(me + d, tiles)
        if d == 1:
            strips_sent.append((strip_ref.at[pl.ds(0, RIM)], 10, back))
            strips_sent.append((strip_ref.at[pl.ds(RIM, RIM)], 11, ahead))
        sides_sent.append((ct_ref.at[pl.ds(0, RIM)], d - 1, back))
        sides_sent.append((ct_ref.at[pl.ds(SIDE - RIM, RIM)], REACH + d - 1, ahead))

    def launch(copies):
        started = []
        for source, at, peer in copies:
            copy = remote(source, recv_ref.at[at], send_sem.at[at], recv_sem.at[at], {"tile": peer})
            copy.start()
            started.append(copy)
        return started

    strips_sent = launch(strips_sent)
    sides_sent = launch(sides_sent)

    tissue = tissue_ref[...].astype(F32)
    spread_rows = jnp.concatenate(
        [jnp.broadcast_to(tissue[t : t + 1], (SIDE, SIDE * SIDE)) for t in range(SLOTS)], axis=0
    )
    r_at, n_at = iota(spread_rows.shape, 0), iota(spread_rows.shape, 1)
    spread_rows = jnp.where(r_at % SIDE == n_at // SIDE, spread_rows, 0.0).astype(BF16)
    k_at, n_at = iota((SIDE, SIDE * SIDE), 0), iota((SIDE, SIDE * SIDE), 1)
    tissue_t = mm_nt(onehot(k_at == n_at % SIDE), spread_rows)
    for w in range(SIDE):
        ts_ref[w] = tissue_t[w : w + 1]

    for w in range(0, SIDE, 4):
        part = jnp.transpose(up_stream_ref[:, C * w : C * (w + 4)])
        for i in range(4):
            ut_ref[w + i] = part[C * i : C * (i + 1)]

    taps_t = jnp.transpose(dw_ref[...]).astype(BF16)
    k_at, n_at = iota((KS * KS, BAND), 0), iota((KS * KS, BAND), 1)
    col_at = (n_at % TAPW) // GROUP
    place = onehot((col_at < KS) & (k_at == KS * (n_at // TAPW) + col_at))
    taps = mm(taps_t, place)
    r_at, n_at = iota((GROUP, BAND), 0), iota((GROUP, BAND), 1)
    diagonal = r_at == n_at % GROUP
    for g in range(GROUPS):
        first = jnp.where(diagonal, taps[GROUP * g : GROUP * (g + 1)], 0.0).astype(BF16)
        band_ref[g, :GROUP, :] = first
        for w in range(1, BLOCK):
            band_ref[g, GROUP * w : GROUP * (w + 1), :] = pltpu.roll(first, GROUP * w, 1)

    lane = iota((1, LANES), 1)
    slot_of, row_of = lane // SIDE, lane % SIDE

    def per_tile(direction, rule):
        out = []
        for t in range(SLOTS):
            n = nb_ref[t, direction]
            out.append(jnp.where(n >= 0, rule(jnp.maximum(n, 0)), -1))
        return out

    def spread(values, shift):
        result = jnp.full((1, LANES), -1, jnp.int32)
        for t in range(SLOTS):
            result = jnp.where(slot_of == (t + shift) % SLOTS, values[t], result)
        return result

    def add_row(index, row):
        return jnp.where(index >= 0, index + row, -1)

    top = row_of >= SIDE - RIM
    bottom = row_of < RIM

    def own_rule(n):
        return jnp.where(n // SLOTS == me, (n % SLOTS) * SIDE, -1)

    def other_rule(n):
        return jnp.where(n // SLOTS == me, -1, n % SLOTS)

    own_above = spread(per_tile(0, own_rule), -1)
    own_below = spread(per_tile(1, own_rule), 1)
    own = add_row(jnp.where(top, own_above, jnp.where(bottom, own_below, -1)), row_of)
    select_own = onehot(iota((LANES, LANES), 0) == own)
    for w in range(0, SIDE, 8):
        near = mm(jnp.concatenate([ct_ref[w + i] for i in range(8)], axis=0), select_own).astype(BF16)
        for i in range(8):
            ht_ref[w + i] = near[C * i : C * (i + 1)]

    far_above = spread(per_tile(0, other_rule), -1)
    far_below = spread(per_tile(1, other_rule), 1)
    far = jnp.where(
        top,
        jnp.where(far_above >= 0, (row_of - (SIDE - RIM)) * SLOTS + far_above, -1),
        jnp.where(bottom & (far_below >= 0), (RIM + row_of) * SLOTS + far_below, -1),
    )
    k_at = iota((2 * RIM * LANES, LANES), 0)
    far_base = onehot((k_at // LANES) * SLOTS + k_at % SLOTS == far)
    col_of = (k_at % LANES) // SLOTS

    up_w = up_ref[...]
    down_t = down_t_ref[...]
    up_t = jnp.transpose(up_w)
    down_w = jnp.transpose(down_t)
    gain = column(gain_ref[...], LANES)
    scale = column(scale_ref[...], LANES)
    gain = jnp.concatenate([gain] * 4, axis=1)
    scale = jnp.concatenate([scale] * 4, axis=1)
    acc_ref[...] = jnp.zeros_like(acc_ref)
    gg_ref[...] = jnp.zeros_like(gg_ref)
    gs_ref[...] = jnp.zeros_like(gs_ref)

    for copy in strips_sent:
        copy.wait()
    strips = jnp.concatenate(
        [recv_ref[11, i] for i in range(RIM)] + [recv_ref[10, i] for i in range(RIM)], axis=1
    )
    for w in range(0, SIDE, 4):
        select_far = jnp.concatenate(
            [jnp.where(col_of == w + i, far_base, jnp.zeros_like(far_base)) for i in range(4)], axis=1
        )
        got = mm(strips, select_far).astype(BF16)
        for i in range(4):
            ht_ref[w + i] = ht_ref[w + i] + got[:, LANES * i : LANES * (i + 1)]

    def fill(at, centre, halo):
        for a in range(KS):
            s = a - RIM
            if s > 0:
                value = pltpu.roll(jnp.where(row_of < s, halo, centre), LANES - s, 1)
            elif s < 0:
                value = pltpu.roll(jnp.where(row_of >= SIDE + s, halo, centre), -s, 1)
            else:
                value = centre
            pt_ref[a, at] = value

    def fill_step(w, carry):
        fill(RIM + w, ct_ref[w], ht_ref[w])
        return carry

    lax.fori_loop(0, SIDE, fill_step, 0, unroll=FILL_UNROLL)

    def window(g, blocks):
        return jnp.concatenate(
            [
                jnp.concatenate(
                    [
                        pt_ref[a, BLOCK * j : BLOCK * j + TAPW // GROUP, GROUP * g : GROUP * (g + 1)].reshape(
                            TAPW, LANES
                        )
                        for a in range(KS)
                    ],
                    axis=0,
                )
                for j in blocks
            ],
            axis=1,
        )

    def fold(values):
        total = values[:, :LANES]
        for j in range(1, values.shape[1] // LANES):
            total = total + values[:, LANES * j : LANES * (j + 1)]
        return total

    def work(blocks):
        for g in range(GROUPS):
            out = mm(band_ref[g], window(g, blocks))
            for w in range(BLOCK):
                mixed_ref[w, GROUP * g : GROUP * (g + 1), :] = out[GROUP * w : GROUP * (w + 1)]

        def step(i, carry):
            columns = [(2 * i + v, j) for v in range(2) for j in blocks]

            def gather(ref):
                return jnp.concatenate([ref[BLOCK * j + w] for w, j in columns], axis=1)

            mixed = jnp.concatenate([mixed_ref[2 * i], mixed_ref[2 * i + 1]], axis=1)
            mean = jnp.sum(mixed, axis=0, keepdims=True) * (1.0 / C)
            centered = mixed - mean
            inverse = lax.rsqrt(jnp.sum(centered * centered, axis=0, keepdims=True) * (1.0 / C) + EPS)
            normed = centered * inverse
            lowered = (normed * gain).astype(BF16)
            hidden = mm(up_t, lowered)
            active, steepness = gelu_parts(hidden)
            active = active.astype(BF16)
            branch = mm(down_t, active)
            tissue = gather(ts_ref)
            summed = gather(ct_ref).astype(F32) + scale * branch
            features = (summed * tissue).astype(BF16)
            grad_out = gather(ut_ref).astype(F32) * (tissue * loss_factor)
            gs_ref[...] += fold(grad_out * branch)
            grad_branch = (grad_out * scale).astype(BF16)
            acc_ref[0] += mm_nt(active, grad_branch)
            grad_active = mm(down_w, grad_branch)
            grad_hidden = (grad_active * steepness).astype(BF16)
            acc_ref[1] += mm_nt(grad_hidden, lowered)
            grad_lowered = mm(up_w, grad_hidden)
            gg_ref[...] += fold(grad_lowered * normed)
            scaled = grad_lowered * gain
            mean_one = jnp.sum(scaled, axis=0, keepdims=True) * (1.0 / C)
            mean_two = jnp.sum(scaled * normed, axis=0, keepdims=True) * (1.0 / C)
            grad_mixed = (inverse * (scaled - mean_one - normed * mean_two)).astype(BF16)
            for at, (w, j) in enumerate(columns):
                lanes = slice(LANES * at, LANES * (at + 1))
                gm_ref[w, :, LANES * j : LANES * (j + 1)] = grad_mixed[:, lanes]
                ft_ref[BLOCK * j + w] = features[:, lanes]
            return carry

        lax.fori_loop(0, BLOCK // 2, step, 0, unroll=STEP_UNROLL)

    work((1, 2))

    for copy in sides_sent:
        copy.wait()
    for east in (0, 1):
        def rule(n, east=east):
            away = n // SLOTS - me
            away = away if east else -away
            return away * LANES + (n % SLOTS) * SIDE

        straight = spread(per_tile(2 + east, rule), 0)
        above = spread(per_tile(4 + east, rule), -1)
        below = spread(per_tile(6 + east, rule), 1)
        halo = jnp.where(top, above, jnp.where(bottom, below, -1))
        index = jnp.concatenate([add_row(straight, row_of), add_row(halo, row_of)], axis=1)
        select = onehot(iota(((REACH + 1) * LANES, 2 * LANES), 0) == index)
        first = 0 if east else SIDE - RIM
        base = 0 if east else REACH
        source = jnp.concatenate(
            [
                jnp.concatenate(
                    [ct_ref[first + i]] + [recv_ref[base + d, i] for d in range(REACH)], axis=1
                )
                for i in range(RIM)
            ],
            axis=0,
        )
        sides = mm(source, select).astype(BF16)
        for i in range(RIM):
            side_ref[east * RIM + i] = sides[C * i : C * (i + 1)]

    for i in range(RIM):
        for east in (0, 1):
            both = side_ref[east * RIM + i]
            fill(east * (RIM + SIDE) + i, both[:, :LANES], both[:, LANES:])

    work((0, 3))

    def pieces(values):
        filled = jnp.concatenate([values, jnp.zeros((HID, 128 - C), F32)], axis=1)
        out = []
        for i in range(PLANE):
            piece = filled[PIECE * i : PIECE * (i + 1)]
            out.append(jnp.concatenate([piece, jnp.zeros((PIECE_PAD - PIECE, 128), F32)], axis=0))
        return out

    for half in range(2):
        for i, piece in enumerate(pieces(acc_ref[half])):
            big_ref[half, i] = piece.astype(BF16)
    to_core = remote(big_ref.at[1 - core], core_in, sum_send.at[0], sum_recv.at[0], partner)
    to_core.start()

    def gradient(g):
        left = jnp.concatenate([gm_ref[w, GROUP * g : GROUP * (g + 1), :] for w in range(BLOCK)], axis=0)
        full = mm_nt(left, window(g, range(BLOCKS)))
        total = None
        for w in range(BLOCK):
            part = jnp.where(diagonal, full[GROUP * w : GROUP * (w + 1)], 0.0)
            if w:
                part = pltpu.roll(part, BAND - GROUP * w, 1)
            total = part if total is None else total + part
        return total

    totals = [gradient(g) for g in range(GROUPS // 2)]

    to_core.wait()
    for i in range(PLANE):
        rs_src[i] = (big_ref[core, i].astype(F32) + core_in[i].astype(F32)).astype(BF16)

    def scatter(target, source, at):
        for k in range(1, PLANE):
            i, device = plane_peer(k)
            remote(source(i), target(k), sum_send.at[at], sum_recv.at[at], device).start()

    def settle(ref, count, at):
        block = ref.at[pl.ds(0, count)]
        copy = remote(block, block, sum_send.at[at], sum_recv.at[at], partner)
        copy.wait()

    scatter(lambda k: rs_in.at[k], lambda i: rs_src.at[i], 1)

    totals += [gradient(g) for g in range(GROUPS // 2, GROUPS)]
    totals = jnp.concatenate(totals, axis=0).astype(BF16)
    k_at, n_at = iota((BAND, LANES), 0), iota((BAND, LANES), 1)
    col_at = (k_at % TAPW) // GROUP
    place = onehot((col_at < KS) & (n_at == KS * (k_at // TAPW) + col_at))
    small = mm(totals, place)
    n_at = iota((C, LANES), 1)
    small = jnp.where(n_at == KS * KS, jnp.sum(gg_ref[...], axis=1, keepdims=True), small)
    small = jnp.where(n_at == KS * KS + 1, jnp.sum(gs_ref[...], axis=1, keepdims=True), small)
    small = jnp.concatenate([small[: C // 2, :64], small[C // 2 :, :64]], axis=1).astype(BF16)
    small_core[core] = small
    small_to_core = remote(
        small_core.at[core], small_core.at[core], sum_send.at[2], sum_recv.at[2], partner
    )
    small_to_core.start()
    small_to_core.wait()
    small = (small_core[0].astype(F32) + small_core[1].astype(F32)).astype(BF16)
    small_plane[me_plane] = small
    scatter(lambda k: small_plane.at[me_plane], lambda i: small_plane.at[me_plane], 3)

    settle(rs_in, PLANE - 1, 1)
    total = rs_src[me_plane].astype(F32)
    for k in range(1, PLANE):
        total = total + rs_in[k].astype(F32)
    y_buf[me_y] = total.astype(BF16)
    for k in range(1, 4):
        remote(y_buf.at[me_y], y_buf.at[me_y], sum_send.at[4], sum_recv.at[4], y_peer(k)).start()

    settle(small_plane, PLANE - 1, 3)
    total = small_plane[0].astype(F32)
    for k in range(1, PLANE):
        total = total + small_plane[k].astype(F32)
    small_y[me_y] = total.astype(BF16)
    for k in range(1, 4):
        remote(small_y.at[me_y], small_y.at[me_y], sum_send.at[5], sum_recv.at[5], y_peer(k)).start()

    settle(y_buf, 3, 4)
    total = y_buf[0].astype(F32)
    for k in range(1, 4):
        total = total + y_buf[k].astype(F32)
    ag_buf[core, me_plane] = total.astype(BF16)
    scatter(lambda k: ag_buf.at[core, me_plane], lambda i: ag_buf.at[core, me_plane], 6)

    for w in range(0, SIDE, 4):
        part = jnp.concatenate([ft_ref[w + i] for i in range(4)], axis=0)
        feat_ref[:, C * w : C * (w + 4)] = jnp.transpose(part)

    settle(small_y, 3, 5)
    total = small_y[0].astype(F32)
    for k in range(1, 4):
        total = total + small_y[k].astype(F32)
    total = jnp.concatenate([total[:, :64], total[:, 64:]], axis=0)
    total = jnp.transpose(jnp.concatenate([total, jnp.zeros((C, 64), F32)], axis=1))
    out_dw_ref[...] = total[: KS * KS]
    out_gain_ref[...] = total[KS * KS : KS * KS + 1]
    out_scale_ref[...] = total[KS * KS + 1 : KS * KS + 2]

    settle(ag_buf.at[core], PLANE - 1, 6)
    last = remote(ag_buf.at[core], ag_buf.at[core], sum_send.at[7], sum_recv.at[7], partner)
    last.start()
    last.wait()
    for half, ref in ((0, out_down_ref), (1, out_up_ref)):
        joined = jnp.concatenate([ag_buf[half, i].astype(F32)[:PIECE] for i in range(PLANE)], axis=0)
        ref[...] = jnp.transpose(joined)[:C]


def vmem(count):
    return [pl.BlockSpec(memory_space=pltpu.VMEM)] * count


def local(
    pixels,
    tissue,
    neighbours,
    upstream,
    stem_weight,
    stem_gain,
    dw_weight,
    norm_gain,
    up_weight,
    down_weight,
    layer_scale,
):
    tiles = lax.axis_size("tile")
    loss_factor = (tiles * lax.axis_size("slab") * SLOTS * SIDE * SIDE) ** (-0.5)
    dma = pltpu.SemaphoreType.DMA
    features, grad_dw, grad_gain, grad_up, grad_down_t, grad_scale = pl.pallas_call(
        functools.partial(whole_kernel, tiles, loss_factor),
        out_shape=(
            jax.ShapeDtypeStruct((LANES, SIDE * C), BF16),
            jax.ShapeDtypeStruct((KS * KS, C), F32),
            jax.ShapeDtypeStruct((1, C), F32),
            jax.ShapeDtypeStruct((C, HID), F32),
            jax.ShapeDtypeStruct((C, HID), F32),
            jax.ShapeDtypeStruct((1, C), F32),
        ),
        in_specs=[pl.BlockSpec(memory_space=pltpu.SMEM)] + vmem(10),
        out_specs=tuple(vmem(6)),
        scratch_shapes=[
            pltpu.VMEM((SIDE, C, LANES), BF16),
            pltpu.VMEM((2 * RIM, C, LANES), BF16),
            pltpu.VMEM((2 * REACH + 2, RIM, C, LANES), BF16),
            pltpu.VMEM((KS, PADW, C, LANES), BF16),
            pltpu.VMEM((SIDE, C, LANES), BF16),
            pltpu.VMEM((2 * RIM, C, 2 * LANES), BF16),
            pltpu.VMEM((GROUPS, BLOCK * GROUP, BAND), BF16),
            pltpu.VMEM((BLOCK, C, 2 * LANES), F32),
            pltpu.VMEM((BLOCK, C, BLOCKS * LANES), BF16),
            pltpu.VMEM((SIDE, C, LANES), BF16),
            pltpu.VMEM((SIDE, C, LANES), BF16),
            pltpu.VMEM((SIDE, 1, LANES), F32),
            pltpu.VMEM((2, HID, C), F32),
            pltpu.VMEM((C, LANES), F32),
            pltpu.VMEM((C, LANES), F32),
            pltpu.VMEM((2, PLANE, PIECE_PAD, 128), BF16),
            pltpu.VMEM((PLANE, PIECE_PAD, 128), BF16),
            pltpu.VMEM((PLANE, PIECE_PAD, 128), BF16),
            pltpu.VMEM((PLANE, PIECE_PAD, 128), BF16),
            pltpu.VMEM((4, PIECE_PAD, 128), BF16),
            pltpu.VMEM((2, PLANE, PIECE_PAD, 128), BF16),
            pltpu.VMEM((2, C // 2, 128), BF16),
            pltpu.VMEM((PLANE, C // 2, 128), BF16),
            pltpu.VMEM((4, C // 2, 128), BF16),
            dma((2 * REACH + 2,)),
            dma((2 * REACH + 2,)),
            dma((8,)),
            dma((8,)),
        ],
        compiler_params=pltpu.CompilerParams(
            collective_id=0, has_side_effects=True, vmem_limit_bytes=56 * 1024 * 1024
        ),
        name="whole",
    )(
        neighbours[0],
        pixels[0],
        stem_weight,
        stem_gain[None],
        upstream.reshape(LANES, SIDE * C),
        tissue[0],
        dw_weight,
        norm_gain[None],
        up_weight,
        down_weight.T,
        layer_scale[None],
    )
    return (
        features.reshape(upstream.shape),
        grad_dw,
        grad_gain[0],
        grad_up,
        grad_down_t.T,
        grad_scale[0],
    )


def solution(mesh):
    placed = (
        P("slab", "tile", None, None),
        P("slab", "tile", None),
        P("slab", "tile", None),
        P("slab", "tile", None, None),
        P(),
        P(),
        P(),
        P(),
        P(),
        P(),
        P(),
    )
    return jax.shard_map(
        local,
        mesh=mesh,
        in_specs=placed,
        out_specs=(P("slab", "tile", None, None), P(), P(), P(), P(), P()),
        check_vma=False,
    )
```

```python
import functools

import jax
import jax.numpy as jnp
from jax import lax
from jax.experimental import pallas as pl
from jax.experimental.pallas import tpu as pltpu
from jax.sharding import PartitionSpec as P

MESH = pl.DeviceIdType.MESH
C = 96
HID = 384
PATCH = 4
KS = 7
SIDE = 32
RIM = 3
REACH = 5
SLOTS = 4
LANES = SLOTS * SIDE
PADW = SIDE + 2 * RIM
GROUP = 16
GROUPS = C // GROUP
BLOCK = 8
BLOCKS = SIDE // BLOCK
TAPW = (BLOCK + RIM * 2) * GROUP
BAND = KS * TAPW
EPS = 1e-06
VMEM_BYTES = 56 * 1024 * 1024
FILL_UNROLL = 32
PLANE = 16
PIECE = HID // PLANE
PIECE_PAD = 32

BF16 = jnp.bfloat16
F32 = jnp.float32


def iota(shape, dim):
    return lax.broadcasted_iota(jnp.int32, shape, dim)


def onehot(mask):
    return jnp.where(mask, 1.0, 0.0).astype(BF16)


def mm(a, b):
    return lax.dot_general(a, b, (((1,), (0,)), ((), ())), preferred_element_type=F32)


def mm_nt(a, b):
    return lax.dot_general(a, b, (((1,), (1,)), ((), ())), preferred_element_type=F32)


def column(row, lanes):
    return jnp.transpose(jnp.broadcast_to(row, (lanes, row.shape[1])))


def gelu_parts(hidden):
    normal_cdf = 0.5 * (1.0 + lax.erf(hidden * 0.7071067811865476))
    density = jnp.exp(-0.5 * hidden * hidden) * 0.3989422804014327
    return (hidden * normal_cdf, normal_cdf + hidden * density)


def remote(source, target, send_sem, recv_sem, device):
    return pltpu.make_async_remote_copy(
        src_ref=source,
        dst_ref=target,
        send_sem=send_sem,
        recv_sem=recv_sem,
        device_id=device,
        device_id_type=MESH,
    )


def whole_kernel(
    tiles,
    loss_factor,
    nb_ref,
    *refs,
):
    inputs, refs = refs[:10], refs[10:]
    (feat_ref, ag_out, small_out), refs = refs[:3], refs[3:]
    held, refs = refs[:10], refs[10:]
    (
        pix_ref,
        stem_ref,
        stem_gain_ref,
        up_vmem,
        tissue_ref,
        dw_ref,
        gain_ref,
        up_ref,
        down_t_ref,
        scale_ref,
    ) = held
    (
        feat_vmem,
        ag_buf,
        small_ref,
        ct_ref,
        strip_ref,
        strip_in,
        recv_ref,
        pt_ref,
        ht_ref,
        side_ref,
        band_ref,
        mixed_ref,
        gm_ref,
        ut_ref,
        ft_ref,
        ts_ref,
        acc_ref,
        gg_ref,
        gs_ref,
        big_ref,
        core_in,
        rs_src,
        rs_in,
        y_buf,
        small_core,
        small_plane,
        small_y,
        send_sem,
        recv_sem,
        sum_send,
        sum_recv,
        local_sem,
    ) = refs
    me = lax.axis_index("tile")
    slab = lax.axis_index("slab")
    core = slab % 2
    y_hi = slab // 2
    me_plane = me % PLANE
    y_lo = me // PLANE
    me_y = y_lo + 2 * y_hi

    fetches = [
        pltpu.make_async_copy(there, here, local_sem.at[i])
        for i, (there, here) in enumerate(zip(inputs, held))
    ]
    for copy in fetches:
        copy.start()
    partner = {"tile": me, "slab": 2 * y_hi + (1 - core)}

    def plane_peer(k):
        i = lax.rem(me_plane + k, PLANE)
        return i, {"tile": y_lo * PLANE + i, "slab": slab}

    def y_peer(k):
        other_lo = lax.rem(y_lo + k % 2, 2)
        other_hi = lax.rem(y_hi + k // 2, 2)
        return {"tile": other_lo * PLANE + me_plane, "slab": 2 * other_hi + core}

    barrier = pltpu.get_barrier_semaphore()
    greeted = [
        {"tile": lax.rem(me + sign * d + tiles, tiles)} for d in range(1, REACH + 1) for sign in (-1, 1)
    ]
    greeted += [partner]
    greeted += [plane_peer(k)[1] for k in range(1, PLANE)]
    greeted += [y_peer(k) for k in range(1, 4)]
    for device in greeted:
        pl.semaphore_signal(barrier, inc=1, device_id=device, device_id_type=MESH)

    for copy in fetches[:3]:
        copy.wait()
    pix = pix_ref[...].reshape(SLOTS * SIDE * PATCH, SIDE * PATCH * 3)
    rows = SLOTS * SIDE * PATCH
    k_at, n_at = iota((rows, rows), 0), iota((rows, rows), 1)
    pick = onehot(k_at == PATCH * (n_at % LANES) + n_at // LANES)
    pix_t = mm(jnp.transpose(pix), pick).astype(BF16)

    q = PATCH * 3
    wt = jnp.transpose(stem_ref[...])
    k_at, n_at = iota((PATCH * q, PATCH * 4 * q), 0), iota((PATCH * q, PATCH * 4 * q), 1)
    spread_q = onehot((k_at // q == n_at // (4 * q)) & (k_at % q == n_at % q))
    wide = mm(wt, spread_q)
    wide = jnp.concatenate([wide] * 4, axis=0)
    r_at, n_at = iota(wide.shape, 0), iota(wide.shape, 1)
    block_w = jnp.where(r_at // C == (n_at % (4 * q)) // q, wide, 0.0).astype(BF16)

    stem_gain = column(stem_gain_ref[...], LANES)
    eight = SIDE // 4
    operand = jnp.concatenate(
        [
            jnp.concatenate(
                [pix_t[4 * q * g : 4 * q * (g + 1), LANES * pr : LANES * (pr + 1)] for pr in range(PATCH)],
                axis=0,
            )
            for g in range(eight)
        ],
        axis=1,
    )
    raw = mm(block_w, operand)
    for v in range(4):
        part = raw[C * v : C * (v + 1)]
        mean = jnp.sum(part, axis=0, keepdims=True) * (1.0 / C)
        part = part - mean
        inverse = lax.rsqrt(jnp.sum(part * part, axis=0, keepdims=True) * (1.0 / C) + EPS)
        part = part * inverse
        for g in range(eight):
            ct_ref[4 * g + v] = (part[:, LANES * g : LANES * (g + 1)] * stem_gain).astype(BF16)

    tiles_here = 0
    for t in range(SLOTS):
        any_side = nb_ref[t, 0]
        for direction in range(1, 8):
            any_side = jnp.maximum(any_side, nb_ref[t, direction])
        tiles_here = tiles_here + jnp.where(any_side >= 0, 1, 0)
    k_at, n_at = iota((LANES, 2 * LANES), 0), iota((LANES, 2 * LANES), 1)
    lower = n_at >= LANES
    kind = (n_at % LANES) // SIDE
    base = onehot(
        (kind < RIM)
        & (k_at // SIDE == jnp.where(lower, tiles_here - 1, 0))
        & (k_at % SIDE == jnp.where(lower, SIDE - RIM + kind, kind))
    )
    col_of = n_at % SIDE
    packed = jnp.zeros((C, 2 * LANES), F32)
    for w in range(0, SIDE, 8):
        left = jnp.concatenate([ct_ref[w + i] for i in range(8)], axis=1)
        right = jnp.concatenate(
            [jnp.where(col_of == w + i, base, jnp.zeros_like(base)) for i in range(8)], axis=0
        )
        packed = packed + mm(left, right)
    for i in range(2):
        strip_ref[i] = packed[:, LANES * i : LANES * (i + 1)].astype(BF16)

    pl.semaphore_wait(barrier, len(greeted))
    strips_sent, sides_sent = [], []
    for d in range(1, REACH + 1):
        back = lax.rem(me - d + tiles, tiles)
        ahead = lax.rem(me + d, tiles)
        if d == 1:
            strips_sent.append((strip_ref.at[0], strip_in.at[0], 10, back))
            strips_sent.append((strip_ref.at[1], strip_in.at[1], 11, ahead))
        sides_sent.append((ct_ref.at[pl.ds(0, RIM)], recv_ref.at[d - 1], d - 1, back))
        at = REACH + d - 1
        sides_sent.append((ct_ref.at[pl.ds(SIDE - RIM, RIM)], recv_ref.at[at], at, ahead))

    def launch(copies):
        started = []
        for source, target, at, peer in copies:
            copy = remote(source, target, send_sem.at[at], recv_sem.at[at], {"tile": peer})
            copy.start()
            started.append(copy)
        return started

    strips_sent = launch(strips_sent)
    sides_sent = launch(sides_sent)

    for copy in fetches[3:]:
        copy.wait()
    tissue = tissue_ref[...].astype(F32)
    spread_rows = jnp.concatenate(
        [jnp.broadcast_to(tissue[t : t + 1], (SIDE, SIDE * SIDE)) for t in range(SLOTS)], axis=0
    )
    r_at, n_at = iota(spread_rows.shape, 0), iota(spread_rows.shape, 1)
    spread_rows = jnp.where(r_at % SIDE == n_at // SIDE, spread_rows, 0.0).astype(BF16)
    k_at, n_at = iota((SIDE, SIDE * SIDE), 0), iota((SIDE, SIDE * SIDE), 1)
    tissue_t = mm_nt(onehot(k_at == n_at % SIDE), spread_rows)
    for w in range(SIDE):
        ts_ref[w] = tissue_t[w : w + 1]

    for w in range(0, SIDE, 4):
        part = jnp.transpose(up_vmem[:, C * w : C * (w + 4)])
        for i in range(4):
            ut_ref[w + i] = part[C * i : C * (i + 1)]

    taps_t = jnp.transpose(dw_ref[...]).astype(BF16)
    k_at, n_at = iota((KS * KS, BAND), 0), iota((KS * KS, BAND), 1)
    col_at = (n_at % TAPW) // GROUP
    place = onehot((col_at < KS) & (k_at == KS * (n_at // TAPW) + col_at))
    taps = mm(taps_t, place)
    r_at, n_at = iota((GROUP, BAND), 0), iota((GROUP, BAND), 1)
    diagonal = r_at == n_at % GROUP
    for g in range(GROUPS):
        first = jnp.where(diagonal, taps[GROUP * g : GROUP * (g + 1)], 0.0).astype(BF16)
        band_ref[g, :GROUP, :] = first
        for w in range(1, BLOCK):
            band_ref[g, GROUP * w : GROUP * (w + 1), :] = pltpu.roll(first, GROUP * w, 1)

    lane = iota((1, LANES), 1)
    slot_of, row_of = lane // SIDE, lane % SIDE

    def per_tile(direction, rule):
        out = []
        for t in range(SLOTS):
            n = nb_ref[t, direction]
            out.append(jnp.where(n >= 0, rule(jnp.maximum(n, 0)), -1))
        return out

    def spread(values, shift):
        result = jnp.full((1, LANES), -1, jnp.int32)
        for t in range(SLOTS):
            result = jnp.where(slot_of == (t + shift) % SLOTS, values[t], result)
        return result

    def add_row(index, row):
        return jnp.where(index >= 0, index + row, -1)

    top = row_of >= SIDE - RIM
    bottom = row_of < RIM

    def own_rule(n):
        return jnp.where(n // SLOTS == me, (n % SLOTS) * SIDE, -1)

    def other_rule(n):
        return jnp.where(n // SLOTS == me, -1, 1)

    own_above = spread(per_tile(0, own_rule), -1)
    own_below = spread(per_tile(1, own_rule), 1)
    own = add_row(jnp.where(top, own_above, jnp.where(bottom, own_below, -1)), row_of)
    select_own = onehot(iota((LANES, LANES), 0) == own)
    for w in range(0, SIDE, 8):
        near = mm(jnp.concatenate([ct_ref[w + i] for i in range(8)], axis=0), select_own).astype(BF16)
        for i in range(8):
            ht_ref[w + i] = near[C * i : C * (i + 1)]

    far_above = spread(per_tile(0, other_rule), -1)
    far_below = spread(per_tile(1, other_rule), 1)
    far = jnp.where(
        top & (far_above >= 0),
        row_of - (SIDE - RIM),
        jnp.where(bottom & (far_below >= 0), SLOTS + row_of, -1),
    )
    k_at = iota((2 * LANES, LANES), 0)
    far_base = onehot(k_at // SIDE == far)
    col_of = k_at % SIDE

    up_w = up_ref[...]
    down_t = down_t_ref[...]
    up_t = jnp.transpose(up_w)
    down_w = jnp.transpose(down_t)
    gain = column(gain_ref[...], LANES)
    scale = column(scale_ref[...], LANES)
    gain = jnp.concatenate([gain] * 4, axis=1)
    scale = jnp.concatenate([scale] * 4, axis=1)
    acc_ref[...] = jnp.zeros_like(acc_ref)
    gg_ref[...] = jnp.zeros_like(gg_ref)
    gs_ref[...] = jnp.zeros_like(gs_ref)

    for copy in strips_sent:
        copy.wait()
    strips = jnp.concatenate([strip_in[1], strip_in[0]], axis=1)
    for w in range(0, SIDE, 4):
        select_far = jnp.concatenate(
            [jnp.where(col_of == w + i, far_base, jnp.zeros_like(far_base)) for i in range(4)], axis=1
        )
        got = mm(strips, select_far).astype(BF16)
        for i in range(4):
            ht_ref[w + i] = ht_ref[w + i] + got[:, LANES * i : LANES * (i + 1)]

    def fill(at, centre, halo):
        for a in range(KS):
            s = a - RIM
            if s > 0:
                value = pltpu.roll(jnp.where(row_of < s, halo, centre), LANES - s, 1)
            elif s < 0:
                value = pltpu.roll(jnp.where(row_of >= SIDE + s, halo, centre), -s, 1)
            else:
                value = centre
            pt_ref[a, at] = value

    def fill_step(w, carry):
        fill(RIM + w, ct_ref[w], ht_ref[w])
        return carry

    lax.fori_loop(0, SIDE, fill_step, 0, unroll=FILL_UNROLL)

    def window(g, blocks):
        return jnp.concatenate(
            [
                jnp.concatenate(
                    [
                        pt_ref[a, BLOCK * j : BLOCK * j + TAPW // GROUP, GROUP * g : GROUP * (g + 1)].reshape(
                            TAPW, LANES
                        )
                        for a in range(KS)
                    ],
                    axis=0,
                )
                for j in blocks
            ],
            axis=1,
        )

    def fold(values):
        total = values[:, :LANES]
        for j in range(1, values.shape[1] // LANES):
            total = total + values[:, LANES * j : LANES * (j + 1)]
        return total

    def work(blocks, defer):
        for g in range(GROUPS):
            out = mm(band_ref[g], window(g, blocks))
            for w in range(BLOCK):
                mixed_ref[w, GROUP * g : GROUP * (g + 1), :] = out[GROUP * w : GROUP * (w + 1)]

        def pair_of(i):
            return [(2 * i + v, j) for v in range(2) for j in blocks]

        def gather(ref, i):
            return jnp.concatenate([ref[BLOCK * j + w] for w, j in pair_of(i)], axis=1)

        def front(i):
            tissue = gather(ts_ref, i)
            grad_out = gather(ut_ref, i).astype(F32) * (tissue * loss_factor)
            grad_branch = (grad_out * scale).astype(BF16)
            grad_active = mm(down_w, grad_branch)
            mixed = jnp.concatenate([mixed_ref[2 * i], mixed_ref[2 * i + 1]], axis=1)
            mean = jnp.sum(mixed, axis=0, keepdims=True) * (1.0 / C)
            centered = mixed - mean
            inverse = lax.rsqrt(jnp.sum(centered * centered, axis=0, keepdims=True) * (1.0 / C) + EPS)
            normed = centered * inverse
            lowered = (normed * gain).astype(BF16)
            hidden = mm(up_t, lowered)
            return tissue, grad_out, grad_branch, grad_active, normed, inverse, lowered, hidden

        def middle(state):
            grad_active, hidden = state[3], state[7]
            active, steepness = gelu_parts(hidden)
            return active.astype(BF16), (grad_active * steepness).astype(BF16)

        def large(state, pair):
            active, grad_hidden = pair
            acc_ref[0] += mm_nt(active, state[2])
            acc_ref[1] += mm_nt(grad_hidden, state[6])

        def back(i, state, pair):
            tissue, grad_out, _, _, normed, inverse, _, _ = state
            active, grad_hidden = pair
            grad_lowered = mm(up_w, grad_hidden)
            branch = mm(down_t, active)
            summed = gather(ct_ref, i).astype(F32) + scale * branch
            features = (summed * tissue).astype(BF16)
            gs_ref[...] += fold(grad_out * branch)
            gg_ref[...] += fold(grad_lowered * normed)
            scaled = grad_lowered * gain
            mean_one = jnp.sum(scaled, axis=0, keepdims=True) * (1.0 / C)
            mean_two = jnp.sum(scaled * normed, axis=0, keepdims=True) * (1.0 / C)
            grad_mixed = (inverse * (scaled - mean_one - normed * mean_two)).astype(BF16)
            for at, (w, j) in enumerate(pair_of(i)):
                lanes = slice(LANES * at, LANES * (at + 1))
                gm_ref[w, :, LANES * j : LANES * (j + 1)] = grad_mixed[:, lanes]
                ft_ref[BLOCK * j + w] = features[:, lanes]

        kept = []
        state = front(0)
        for i in range(BLOCK // 2):
            pair = middle(state)
            later = front(i + 1) if i + 1 < BLOCK // 2 else None
            large(state, pair)
            if defer:
                kept.append((i, state, pair))
            else:
                back(i, state, pair)
            state = later

        def finish():
            for i, state, pair in kept:
                back(i, state, pair)

        return finish

    work((1, 2), False)

    for copy in sides_sent:
        copy.wait()
    for east in (0, 1):
        def rule(n, east=east):
            away = n // SLOTS - me
            away = away if east else -away
            return away * LANES + (n % SLOTS) * SIDE

        straight = spread(per_tile(2 + east, rule), 0)
        above = spread(per_tile(4 + east, rule), -1)
        below = spread(per_tile(6 + east, rule), 1)
        halo = jnp.where(top, above, jnp.where(bottom, below, -1))
        index = jnp.concatenate([add_row(straight, row_of), add_row(halo, row_of)], axis=1)
        select = onehot(iota(((REACH + 1) * LANES, 2 * LANES), 0) == index)
        first = 0 if east else SIDE - RIM
        base = 0 if east else REACH
        source = jnp.concatenate(
            [
                jnp.concatenate(
                    [ct_ref[first + i]] + [recv_ref[base + d, i] for d in range(REACH)], axis=1
                )
                for i in range(RIM)
            ],
            axis=0,
        )
        sides = mm(source, select).astype(BF16)
        for i in range(RIM):
            side_ref[east * RIM + i] = sides[C * i : C * (i + 1)]

    for i in range(RIM):
        for east in (0, 1):
            both = side_ref[east * RIM + i]
            fill(east * (RIM + SIDE) + i, both[:, :LANES], both[:, LANES:])

    finish = work((0, 3), True)

    def pieces(values):
        filled = jnp.concatenate([values, jnp.zeros((HID, 128 - C), F32)], axis=1)
        out = []
        for i in range(PLANE):
            piece = filled[PIECE * i : PIECE * (i + 1)]
            out.append(jnp.concatenate([piece, jnp.zeros((PIECE_PAD - PIECE, 128), F32)], axis=0))
        return out

    for half in range(2):
        for i, piece in enumerate(pieces(acc_ref[half])):
            big_ref[half, i] = piece.astype(BF16)
    to_core = remote(big_ref.at[1 - core], core_in, sum_send.at[0], sum_recv.at[0], partner)
    to_core.start()
    finish()

    def gradient(g):
        left = jnp.concatenate([gm_ref[w, GROUP * g : GROUP * (g + 1), :] for w in range(BLOCK)], axis=0)
        full = mm_nt(left, window(g, range(BLOCKS)))
        total = None
        for w in range(BLOCK):
            part = jnp.where(diagonal, full[GROUP * w : GROUP * (w + 1)], 0.0)
            if w:
                part = pltpu.roll(part, BAND - GROUP * w, 1)
            total = part if total is None else total + part
        return total

    totals = [gradient(g) for g in range(GROUPS // 2)]

    to_core.wait()
    for i in range(PLANE):
        rs_src[i] = (big_ref[core, i].astype(F32) + core_in[i].astype(F32)).astype(BF16)

    def scatter(target, source, at):
        for k in range(1, PLANE):
            i, device = plane_peer(k)
            remote(source(i), target(k), sum_send.at[at], sum_recv.at[at], device).start()

    def settle(ref, count, at):
        block = ref.at[pl.ds(0, count)]
        copy = remote(block, block, sum_send.at[at], sum_recv.at[at], partner)
        copy.wait()

    scatter(lambda k: rs_in.at[k], lambda i: rs_src.at[i], 1)

    totals += [gradient(g) for g in range(GROUPS // 2, GROUPS)]
    totals = jnp.concatenate(totals, axis=0).astype(BF16)
    k_at, n_at = iota((BAND, LANES), 0), iota((BAND, LANES), 1)
    col_at = (k_at % TAPW) // GROUP
    place = onehot((col_at < KS) & (n_at == KS * (k_at // TAPW) + col_at))
    small = mm(totals, place)
    n_at = iota((C, LANES), 1)
    small = jnp.where(n_at == KS * KS, jnp.sum(gg_ref[...], axis=1, keepdims=True), small)
    small = jnp.where(n_at == KS * KS + 1, jnp.sum(gs_ref[...], axis=1, keepdims=True), small)
    small = jnp.concatenate([small[: C // 2, :64], small[C // 2 :, :64]], axis=1).astype(BF16)
    small_core[core] = small
    small_to_core = remote(
        small_core.at[core], small_core.at[core], sum_send.at[2], sum_recv.at[2], partner
    )
    small_to_core.start()
    small_to_core.wait()
    small = (small_core[0].astype(F32) + small_core[1].astype(F32)).astype(BF16)
    small_plane[me_plane] = small
    scatter(lambda k: small_plane.at[me_plane], lambda i: small_plane.at[me_plane], 3)

    settle(rs_in, PLANE - 1, 1)
    total = rs_src[me_plane].astype(F32)
    for k in range(1, PLANE):
        total = total + rs_in[k].astype(F32)
    y_buf[me_y] = total.astype(BF16)
    for k in range(1, 4):
        remote(y_buf.at[me_y], y_buf.at[me_y], sum_send.at[4], sum_recv.at[4], y_peer(k)).start()

    settle(small_plane, PLANE - 1, 3)
    total = small_plane[0].astype(F32)
    for k in range(1, PLANE):
        total = total + small_plane[k].astype(F32)
    small_y[me_y] = total.astype(BF16)
    for k in range(1, 4):
        remote(small_y.at[me_y], small_y.at[me_y], sum_send.at[5], sum_recv.at[5], y_peer(k)).start()

    settle(y_buf, 3, 4)
    total = y_buf[0].astype(F32)
    for k in range(1, 4):
        total = total + y_buf[k].astype(F32)
    ag_buf[core, me_plane] = total.astype(BF16)
    scatter(lambda k: ag_buf.at[core, me_plane], lambda i: ag_buf.at[core, me_plane], 6)

    for w in range(0, SIDE, 4):
        part = jnp.concatenate([ft_ref[w + i] for i in range(4)], axis=0)
        feat_vmem[:, C * w : C * (w + 4)] = jnp.transpose(part)
    store = pltpu.make_async_copy(feat_vmem, feat_ref, local_sem.at[10])
    store.start()

    settle(small_y, 3, 5)
    total = small_y[0].astype(F32)
    for k in range(1, 4):
        total = total + small_y[k].astype(F32)
    small_ref[...] = total
    store_small = pltpu.make_async_copy(small_ref, small_out, local_sem.at[11])
    store_small.start()

    settle(ag_buf.at[core], PLANE - 1, 6)
    last = remote(ag_buf.at[core], ag_buf.at[core], sum_send.at[7], sum_recv.at[7], partner)
    last.start()
    last.wait()
    store_sums = pltpu.make_async_copy(ag_buf, ag_out, local_sem.at[12])
    store_sums.start()
    for copy in (store, store_small, store_sums):
        copy.wait()


def finish_kernel(*refs):
    inputs, outputs, refs = refs[:3], refs[3:9], refs[9:]
    (feat, ag_ref, small_ref), refs = refs[:3], refs[3:]
    (dw_ref, gain_ref, up_ref, down_ref, scale_ref), (sem_in, sem_out) = refs[:5], refs[5:]
    coming = [
        pltpu.make_async_copy(there, here, sem_in.at[i])
        for i, (there, here) in enumerate(zip(inputs, (feat, ag_ref, small_ref)))
    ]
    results = (feat, dw_ref, gain_ref, up_ref, down_ref, scale_ref)
    going = [
        pltpu.make_async_copy(here, there, sem_out.at[i])
        for i, (here, there) in enumerate(zip(results, outputs))
    ]
    for copy in coming:
        copy.start()
    coming[2].wait()
    total = small_ref[...]
    total = jnp.concatenate([total[:, :64], total[:, 64:]], axis=0)
    total = jnp.transpose(jnp.concatenate([total, jnp.zeros((C, 64), F32)], axis=1))
    dw_ref[...] = total[: KS * KS]
    gain_ref[...] = total[KS * KS : KS * KS + 1]
    scale_ref[...] = total[KS * KS + 1 : KS * KS + 2]
    for i in (1, 2, 5):
        going[i].start()
    coming[1].wait()
    for half, ref in ((0, down_ref), (1, up_ref)):
        joined = jnp.concatenate([ag_ref[half, i].astype(F32)[:PIECE] for i in range(PLANE)], axis=0)
        ref[...] = jnp.transpose(joined)[:C]
    for i in (3, 4):
        going[i].start()
    coming[0].wait()
    going[0].start()
    for copy in going:
        copy.wait()


def anywhere(count):
    return [pl.BlockSpec(memory_space=pl.ANY)] * count


def local(
    pixels,
    tissue,
    neighbours,
    upstream,
    stem_weight,
    stem_gain,
    dw_weight,
    norm_gain,
    up_weight,
    down_weight,
    layer_scale,
):
    tiles = lax.axis_size("tile")
    loss_factor = (tiles * lax.axis_size("slab") * SLOTS * SIDE * SIDE) ** (-0.5)
    dma = pltpu.SemaphoreType.DMA
    operands = (
        pixels[0],
        stem_weight,
        stem_gain[None],
        upstream.reshape(LANES, SIDE * C),
        tissue[0],
        dw_weight,
        norm_gain[None],
        up_weight,
        down_weight.T,
        layer_scale[None],
    )
    features, gathered, small = pl.pallas_call(
        functools.partial(whole_kernel, tiles, loss_factor),
        out_shape=(
            jax.ShapeDtypeStruct((LANES, SIDE * C), BF16),
            jax.ShapeDtypeStruct((2, PLANE, PIECE_PAD, 128), BF16),
            jax.ShapeDtypeStruct((C // 2, 128), F32),
        ),
        in_specs=[pl.BlockSpec(memory_space=pltpu.SMEM)] + anywhere(10),
        out_specs=tuple(anywhere(3)),
        scratch_shapes=[pltpu.VMEM(x.shape, x.dtype) for x in operands]
        + [
            pltpu.VMEM((LANES, SIDE * C), BF16),
            pltpu.VMEM((2, PLANE, PIECE_PAD, 128), BF16),
            pltpu.VMEM((C // 2, 128), F32),
            pltpu.VMEM((SIDE, C, LANES), BF16),
            pltpu.VMEM((2, C, LANES), BF16),
            pltpu.VMEM((2, C, LANES), BF16),
            pltpu.VMEM((2 * REACH, RIM, C, LANES), BF16),
            pltpu.VMEM((KS, PADW, C, LANES), BF16),
            pltpu.VMEM((SIDE, C, LANES), BF16),
            pltpu.VMEM((2 * RIM, C, 2 * LANES), BF16),
            pltpu.VMEM((GROUPS, BLOCK * GROUP, BAND), BF16),
            pltpu.VMEM((BLOCK, C, 2 * LANES), F32),
            pltpu.VMEM((BLOCK, C, BLOCKS * LANES), BF16),
            pltpu.VMEM((SIDE, C, LANES), BF16),
            pltpu.VMEM((SIDE, C, LANES), BF16),
            pltpu.VMEM((SIDE, 1, LANES), F32),
            pltpu.VMEM((2, HID, C), F32),
            pltpu.VMEM((C, LANES), F32),
            pltpu.VMEM((C, LANES), F32),
            pltpu.VMEM((2, PLANE, PIECE_PAD, 128), BF16),
            pltpu.VMEM((PLANE, PIECE_PAD, 128), BF16),
            pltpu.VMEM((PLANE, PIECE_PAD, 128), BF16),
            pltpu.VMEM((PLANE, PIECE_PAD, 128), BF16),
            pltpu.VMEM((4, PIECE_PAD, 128), BF16),
            pltpu.VMEM((2, C // 2, 128), BF16),
            pltpu.VMEM((PLANE, C // 2, 128), BF16),
            pltpu.VMEM((4, C // 2, 128), BF16),
            dma((2 * REACH + 2,)),
            dma((2 * REACH + 2,)),
            dma((8,)),
            dma((8,)),
            dma((13,)),
        ],
        compiler_params=pltpu.CompilerParams(
            collective_id=0, has_side_effects=True, vmem_limit_bytes=VMEM_BYTES
        ),
        name="whole",
    )(neighbours[0], *operands)
    features, grad_dw, grad_gain, grad_up, grad_down_t, grad_scale = pl.pallas_call(
        finish_kernel,
        out_shape=(
            jax.ShapeDtypeStruct((LANES, SIDE * C), BF16),
            jax.ShapeDtypeStruct((KS * KS, C), F32),
            jax.ShapeDtypeStruct((1, C), F32),
            jax.ShapeDtypeStruct((C, HID), F32),
            jax.ShapeDtypeStruct((C, HID), F32),
            jax.ShapeDtypeStruct((1, C), F32),
        ),
        in_specs=anywhere(3),
        out_specs=tuple(anywhere(6)),
        scratch_shapes=[
            pltpu.VMEM((LANES, SIDE * C), BF16),
            pltpu.VMEM((2, PLANE, PIECE_PAD, 128), BF16),
            pltpu.VMEM((C // 2, 128), F32),
            pltpu.VMEM((KS * KS, C), F32),
            pltpu.VMEM((1, C), F32),
            pltpu.VMEM((C, HID), F32),
            pltpu.VMEM((C, HID), F32),
            pltpu.VMEM((1, C), F32),
            dma((3,)),
            dma((6,)),
        ],
        compiler_params=pltpu.CompilerParams(vmem_limit_bytes=VMEM_BYTES),
        name="finish",
    )(features, gathered, small)
    return (
        features.reshape(upstream.shape),
        grad_dw,
        grad_gain[0],
        grad_up,
        grad_down_t.T,
        grad_scale[0],
    )


def solution(mesh):
    placed = (
        P("slab", "tile", None, None),
        P("slab", "tile", None),
        P("slab", "tile", None),
        P("slab", "tile", None, None),
        P(),
        P(),
        P(),
        P(),
        P(),
        P(),
        P(),
    )
    return jax.shard_map(
        local,
        mesh=mesh,
        in_specs=placed,
        out_specs=(P("slab", "tile", None, None), P(), P(), P(), P(), P()),
        check_vma=False,
    )
```

```python
import functools

import jax
import jax.numpy as jnp
from jax import lax
from jax.experimental import pallas as pl
from jax.experimental.pallas import tpu as pltpu
from jax.sharding import PartitionSpec as P

MESH = pl.DeviceIdType.MESH
C = 96
HID = 384
PATCH = 4
KS = 7
SIDE = 32
RIM = 3
REACH = 5
SLOTS = 4
LANES = SLOTS * SIDE
PADW = SIDE + 2 * RIM
GROUP = 16
GROUPS = C // GROUP
BLOCK = 8
BLOCKS = SIDE // BLOCK
TAPW = (BLOCK + RIM * 2) * GROUP
BAND = KS * TAPW
EPS = 1e-06
VMEM_BYTES = 56 * 1024 * 1024
FILL_UNROLL = 32
PLANE = 16
PIECE = HID // PLANE
PIECE_PAD = 32

BF16 = jnp.bfloat16
F32 = jnp.float32


def iota(shape, dim):
    return lax.broadcasted_iota(jnp.int32, shape, dim)


def onehot(mask):
    return jnp.where(mask, 1.0, 0.0).astype(BF16)


def mm(a, b):
    return lax.dot_general(a, b, (((1,), (0,)), ((), ())), preferred_element_type=F32)


def mm_nt(a, b):
    return lax.dot_general(a, b, (((1,), (1,)), ((), ())), preferred_element_type=F32)


def column(row, lanes):
    return jnp.transpose(jnp.broadcast_to(row, (lanes, row.shape[1])))


def gelu_parts(hidden):
    normal_cdf = 0.5 * (1.0 + lax.erf(hidden * 0.7071067811865476))
    density = jnp.exp(-0.5 * hidden * hidden) * 0.3989422804014327
    return (hidden * normal_cdf, normal_cdf + hidden * density)


def remote(source, target, send_sem, recv_sem, device):
    return pltpu.make_async_remote_copy(
        src_ref=source,
        dst_ref=target,
        send_sem=send_sem,
        recv_sem=recv_sem,
        device_id=device,
        device_id_type=MESH,
    )


def whole_kernel(
    tiles,
    loss_factor,
    nb_ref,
    *refs,
):
    inputs, refs = refs[:10], refs[10:]
    (feat_ref, ag_out, small_out), refs = refs[:3], refs[3:]
    held, refs = refs[:10], refs[10:]
    (
        pix_ref,
        stem_ref,
        stem_gain_ref,
        up_vmem,
        tissue_ref,
        dw_ref,
        gain_ref,
        up_ref,
        down_t_ref,
        scale_ref,
    ) = held
    (
        feat_vmem,
        ag_buf,
        small_ref,
        ct_ref,
        strip_ref,
        strip_in,
        recv_ref,
        pt_ref,
        ht_ref,
        side_ref,
        band_ref,
        mixed_ref,
        gm_ref,
        ut_ref,
        ft_ref,
        ts_ref,
        acc_ref,
        gg_ref,
        gs_ref,
        big_ref,
        core_in,
        rs_src,
        rs_in,
        y_buf,
        dw_part,
        small_plane,
        small_y,
        send_sem,
        recv_sem,
        sum_send,
        sum_recv,
        local_sem,
    ) = refs
    me = lax.axis_index("tile")
    slab = lax.axis_index("slab")
    core = slab % 2
    y_hi = slab // 2
    me_plane = me % PLANE
    y_lo = me // PLANE
    me_y = y_lo + 2 * y_hi

    fetches = [
        pltpu.make_async_copy(there, here, local_sem.at[i])
        for i, (there, here) in enumerate(zip(inputs, held))
    ]
    for copy in fetches:
        copy.start()
    partner = {"tile": me, "slab": 2 * y_hi + (1 - core)}

    def plane_peer(k):
        i = lax.rem(me_plane + k, PLANE)
        return i, {"tile": y_lo * PLANE + i, "slab": slab}

    def y_peer(k, at=core):
        other_lo = lax.rem(y_lo + k % 2, 2)
        other_hi = lax.rem(y_hi + k // 2, 2)
        return {"tile": other_lo * PLANE + me_plane, "slab": 2 * other_hi + at}

    column_peers = [y_peer(k) for k in range(1, 4)] + [y_peer(k, 1 - core) for k in range(4)]

    barrier = pltpu.get_barrier_semaphore()
    greeted = [
        {"tile": lax.rem(me + sign * d + tiles, tiles)} for d in range(1, REACH + 1) for sign in (-1, 1)
    ]
    greeted += [plane_peer(k)[1] for k in range(1, PLANE)]
    greeted += column_peers
    for device in greeted:
        pl.semaphore_signal(barrier, inc=1, device_id=device, device_id_type=MESH)

    for copy in fetches[:3]:
        copy.wait()
    pix = pix_ref[...].reshape(SLOTS * SIDE * PATCH, SIDE * PATCH * 3)
    rows = SLOTS * SIDE * PATCH
    k_at, n_at = iota((rows, rows), 0), iota((rows, rows), 1)
    pick = onehot(k_at == PATCH * (n_at % LANES) + n_at // LANES)
    pix_t = mm(jnp.transpose(pix), pick).astype(BF16)

    q = PATCH * 3
    wt = jnp.transpose(stem_ref[...])
    k_at, n_at = iota((PATCH * q, PATCH * 4 * q), 0), iota((PATCH * q, PATCH * 4 * q), 1)
    spread_q = onehot((k_at // q == n_at // (4 * q)) & (k_at % q == n_at % q))
    wide = mm(wt, spread_q)
    wide = jnp.concatenate([wide] * 4, axis=0)
    r_at, n_at = iota(wide.shape, 0), iota(wide.shape, 1)
    block_w = jnp.where(r_at // C == (n_at % (4 * q)) // q, wide, 0.0).astype(BF16)

    stem_gain = column(stem_gain_ref[...], LANES)
    eight = SIDE // 4
    operand = jnp.concatenate(
        [
            jnp.concatenate(
                [pix_t[4 * q * g : 4 * q * (g + 1), LANES * pr : LANES * (pr + 1)] for pr in range(PATCH)],
                axis=0,
            )
            for g in range(eight)
        ],
        axis=1,
    )
    raw = mm(block_w, operand)
    for v in range(4):
        part = raw[C * v : C * (v + 1)]
        mean = jnp.sum(part, axis=0, keepdims=True) * (1.0 / C)
        part = part - mean
        inverse = lax.rsqrt(jnp.sum(part * part, axis=0, keepdims=True) * (1.0 / C) + EPS)
        part = part * inverse
        for g in range(eight):
            ct_ref[4 * g + v] = (part[:, LANES * g : LANES * (g + 1)] * stem_gain).astype(BF16)

    tiles_here = 0
    for t in range(SLOTS):
        any_side = nb_ref[t, 0]
        for direction in range(1, 8):
            any_side = jnp.maximum(any_side, nb_ref[t, direction])
        tiles_here = tiles_here + jnp.where(any_side >= 0, 1, 0)
    k_at, n_at = iota((LANES, 2 * LANES), 0), iota((LANES, 2 * LANES), 1)
    lower = n_at >= LANES
    kind = (n_at % LANES) // SIDE
    base = onehot(
        (kind < RIM)
        & (k_at // SIDE == jnp.where(lower, tiles_here - 1, 0))
        & (k_at % SIDE == jnp.where(lower, SIDE - RIM + kind, kind))
    )
    col_of = n_at % SIDE
    packed = jnp.zeros((C, 2 * LANES), F32)
    for w in range(0, SIDE, 8):
        left = jnp.concatenate([ct_ref[w + i] for i in range(8)], axis=1)
        right = jnp.concatenate(
            [jnp.where(col_of == w + i, base, jnp.zeros_like(base)) for i in range(8)], axis=0
        )
        packed = packed + mm(left, right)
    for i in range(2):
        strip_ref[i] = packed[:, LANES * i : LANES * (i + 1)].astype(BF16)

    pl.semaphore_wait(barrier, len(greeted))
    strips_sent, sides_sent = [], []
    for d in range(1, REACH + 1):
        back = lax.rem(me - d + tiles, tiles)
        ahead = lax.rem(me + d, tiles)
        if d == 1:
            strips_sent.append((strip_ref.at[0], strip_in.at[0], 10, back))
            strips_sent.append((strip_ref.at[1], strip_in.at[1], 11, ahead))
        if d == REACH:
            sides_sent.append((strip_ref.at[0], strip_in.at[2], d - 1, back))
            sides_sent.append((strip_ref.at[1], strip_in.at[3], REACH + d - 1, ahead))
            continue
        sides_sent.append((ct_ref.at[pl.ds(0, RIM)], recv_ref.at[d - 1], d - 1, back))
        at = REACH + d - 1
        sides_sent.append((ct_ref.at[pl.ds(SIDE - RIM, RIM)], recv_ref.at[at], at, ahead))

    def launch(copies):
        started = []
        for source, target, at, peer in copies:
            copy = remote(source, target, send_sem.at[at], recv_sem.at[at], {"tile": peer})
            copy.start()
            started.append(copy)
        return started

    strips_sent = launch(strips_sent)
    sides_sent = launch(sides_sent)

    for copy in fetches[3:]:
        copy.wait()
    tissue = tissue_ref[...].astype(F32)
    spread_rows = jnp.concatenate(
        [jnp.broadcast_to(tissue[t : t + 1], (SIDE, SIDE * SIDE)) for t in range(SLOTS)], axis=0
    )
    r_at, n_at = iota(spread_rows.shape, 0), iota(spread_rows.shape, 1)
    spread_rows = jnp.where(r_at % SIDE == n_at // SIDE, spread_rows, 0.0).astype(BF16)
    k_at, n_at = iota((SIDE, SIDE * SIDE), 0), iota((SIDE, SIDE * SIDE), 1)
    tissue_t = mm_nt(onehot(k_at == n_at % SIDE), spread_rows)
    for w in range(SIDE):
        ts_ref[w] = tissue_t[w : w + 1]

    for w in range(0, SIDE, 4):
        part = jnp.transpose(up_vmem[:, C * w : C * (w + 4)])
        for i in range(4):
            ut_ref[w + i] = part[C * i : C * (i + 1)]

    taps_t = jnp.transpose(dw_ref[...]).astype(BF16)
    k_at, n_at = iota((KS * KS, BAND), 0), iota((KS * KS, BAND), 1)
    col_at = (n_at % TAPW) // GROUP
    place = onehot((col_at < KS) & (k_at == KS * (n_at // TAPW) + col_at))
    taps = mm(taps_t, place)
    r_at, n_at = iota((GROUP, BAND), 0), iota((GROUP, BAND), 1)
    diagonal = r_at == n_at % GROUP
    for g in range(GROUPS):
        first = jnp.where(diagonal, taps[GROUP * g : GROUP * (g + 1)], 0.0).astype(BF16)
        band_ref[g, :GROUP, :] = first
        for w in range(1, BLOCK):
            band_ref[g, GROUP * w : GROUP * (w + 1), :] = pltpu.roll(first, GROUP * w, 1)

    lane = iota((1, LANES), 1)
    slot_of, row_of = lane // SIDE, lane % SIDE

    def per_tile(direction, rule):
        out = []
        for t in range(SLOTS):
            n = nb_ref[t, direction]
            out.append(jnp.where(n >= 0, rule(jnp.maximum(n, 0)), -1))
        return out

    def spread(values, shift):
        result = jnp.full((1, LANES), -1, jnp.int32)
        for t in range(SLOTS):
            result = jnp.where(slot_of == (t + shift) % SLOTS, values[t], result)
        return result

    def add_row(index, row):
        return jnp.where(index >= 0, index + row, -1)

    top = row_of >= SIDE - RIM
    bottom = row_of < RIM

    def own_rule(n):
        return jnp.where(n // SLOTS == me, (n % SLOTS) * SIDE, -1)

    def other_rule(n):
        return jnp.where(n // SLOTS == me, -1, 1)

    own_above = spread(per_tile(0, own_rule), -1)
    own_below = spread(per_tile(1, own_rule), 1)
    own = add_row(jnp.where(top, own_above, jnp.where(bottom, own_below, -1)), row_of)
    select_own = onehot(iota((LANES, LANES), 0) == own)
    for w in range(0, SIDE, 8):
        near = mm(jnp.concatenate([ct_ref[w + i] for i in range(8)], axis=0), select_own).astype(BF16)
        for i in range(8):
            ht_ref[w + i] = near[C * i : C * (i + 1)]

    far_above = spread(per_tile(0, other_rule), -1)
    far_below = spread(per_tile(1, other_rule), 1)
    far = jnp.where(
        top & (far_above >= 0),
        row_of - (SIDE - RIM),
        jnp.where(bottom & (far_below >= 0), SLOTS + row_of, -1),
    )
    k_at = iota((2 * LANES, LANES), 0)
    far_base = onehot(k_at // SIDE == far)
    col_of = k_at % SIDE

    up_w = up_ref[...]
    down_t = down_t_ref[...]
    up_t = jnp.transpose(up_w)
    down_w = jnp.transpose(down_t)
    gain = column(gain_ref[...], LANES)
    scale = column(scale_ref[...], LANES)
    gain = jnp.concatenate([gain] * 4, axis=1)
    scale = jnp.concatenate([scale] * 4, axis=1)
    acc_ref[...] = jnp.zeros_like(acc_ref)
    gg_ref[...] = jnp.zeros_like(gg_ref)
    gs_ref[...] = jnp.zeros_like(gs_ref)

    for copy in strips_sent:
        copy.wait()
    strips = jnp.concatenate([strip_in[1], strip_in[0]], axis=1)
    for w in range(0, SIDE, 4):
        select_far = jnp.concatenate(
            [jnp.where(col_of == w + i, far_base, jnp.zeros_like(far_base)) for i in range(4)], axis=1
        )
        got = mm(strips, select_far).astype(BF16)
        for i in range(4):
            ht_ref[w + i] = ht_ref[w + i] + got[:, LANES * i : LANES * (i + 1)]

    def fill(at, centre, halo):
        for a in range(KS):
            s = a - RIM
            if s > 0:
                value = pltpu.roll(jnp.where(row_of < s, halo, centre), LANES - s, 1)
            elif s < 0:
                value = pltpu.roll(jnp.where(row_of >= SIDE + s, halo, centre), -s, 1)
            else:
                value = centre
            pt_ref[a, at] = value

    def fill_step(w, carry):
        fill(RIM + w, ct_ref[w], ht_ref[w])
        return carry

    lax.fori_loop(0, SIDE, fill_step, 0, unroll=FILL_UNROLL)

    def window(g, blocks):
        return jnp.concatenate(
            [
                jnp.concatenate(
                    [
                        pt_ref[a, BLOCK * j : BLOCK * j + TAPW // GROUP, GROUP * g : GROUP * (g + 1)].reshape(
                            TAPW, LANES
                        )
                        for a in range(KS)
                    ],
                    axis=0,
                )
                for j in blocks
            ],
            axis=1,
        )

    def fold(values):
        total = values[:, :LANES]
        for j in range(1, values.shape[1] // LANES):
            total = total + values[:, LANES * j : LANES * (j + 1)]
        return total

    def work(blocks, defer):
        for g in range(GROUPS):
            out = mm(band_ref[g], window(g, blocks))
            for w in range(BLOCK):
                mixed_ref[w, GROUP * g : GROUP * (g + 1), :] = out[GROUP * w : GROUP * (w + 1)]

        def pair_of(i):
            return [(2 * i + v, j) for v in range(2) for j in blocks]

        def gather(ref, i):
            return jnp.concatenate([ref[BLOCK * j + w] for w, j in pair_of(i)], axis=1)

        def front(i):
            tissue = gather(ts_ref, i)
            grad_out = gather(ut_ref, i).astype(F32) * (tissue * loss_factor)
            grad_branch = (grad_out * scale).astype(BF16)
            grad_active = mm(down_w, grad_branch)
            mixed = jnp.concatenate([mixed_ref[2 * i], mixed_ref[2 * i + 1]], axis=1)
            mean = jnp.sum(mixed, axis=0, keepdims=True) * (1.0 / C)
            centered = mixed - mean
            inverse = lax.rsqrt(jnp.sum(centered * centered, axis=0, keepdims=True) * (1.0 / C) + EPS)
            normed = centered * inverse
            lowered = (normed * gain).astype(BF16)
            hidden = mm(up_t, lowered)
            return tissue, grad_out, grad_branch, grad_active, normed, inverse, lowered, hidden

        def middle(state):
            grad_active, hidden = state[3], state[7]
            active, steepness = gelu_parts(hidden)
            return active.astype(BF16), (grad_active * steepness).astype(BF16)

        def large(state, pair):
            active, grad_hidden = pair
            acc_ref[0] += mm_nt(active, state[2])
            acc_ref[1] += mm_nt(grad_hidden, state[6])

        def back(i, state, pair):
            tissue, grad_out, _, _, normed, inverse, _, _ = state
            active, grad_hidden = pair
            grad_lowered = mm(up_w, grad_hidden)
            branch = mm(down_t, active)
            summed = gather(ct_ref, i).astype(F32) + scale * branch
            features = (summed * tissue).astype(BF16)
            gs_ref[...] += fold(grad_out * branch)
            gg_ref[...] += fold(grad_lowered * normed)
            scaled = grad_lowered * gain
            mean_one = jnp.sum(scaled, axis=0, keepdims=True) * (1.0 / C)
            mean_two = jnp.sum(scaled * normed, axis=0, keepdims=True) * (1.0 / C)
            grad_mixed = (inverse * (scaled - mean_one - normed * mean_two)).astype(BF16)
            for at, (w, j) in enumerate(pair_of(i)):
                lanes = slice(LANES * at, LANES * (at + 1))
                gm_ref[w, :, LANES * j : LANES * (j + 1)] = grad_mixed[:, lanes]
                ft_ref[BLOCK * j + w] = features[:, lanes]

        kept = []
        state = front(0)
        for i in range(BLOCK // 2):
            pair = middle(state)
            later = front(i + 1) if i + 1 < BLOCK // 2 else None
            large(state, pair)
            if defer:
                kept.append((i, state, pair))
            else:
                back(i, state, pair)
            state = later

        def finish(some):
            for i in some:
                back(*kept[i])

        return finish

    work((1, 2), False)

    def gradient(g, blocks):
        left = jnp.concatenate(
            [
                jnp.concatenate(
                    [gm_ref[w, GROUP * g : GROUP * (g + 1), LANES * j : LANES * (j + 1)] for j in blocks],
                    axis=1,
                )
                for w in range(BLOCK)
            ],
            axis=0,
        )
        full = mm_nt(left, window(g, blocks))
        total = None
        for w in range(BLOCK):
            part = jnp.where(diagonal, full[GROUP * w : GROUP * (w + 1)], 0.0)
            if w:
                part = pltpu.roll(part, BAND - GROUP * w, 1)
            total = part if total is None else total + part
        return total

    for g in range(GROUPS):
        dw_part[g] = gradient(g, (1, 2))

    for copy in sides_sent:
        copy.wait()
    for east in (0, 1):
        def rule(n, east=east):
            away = n // SLOTS - me
            away = away if east else -away
            return away * LANES + (n % SLOTS) * SIDE

        straight = spread(per_tile(2 + east, rule), 0)
        above = spread(per_tile(4 + east, rule), -1)
        below = spread(per_tile(6 + east, rule), 1)
        halo = jnp.where(top, above, jnp.where(bottom, below, -1))
        corner = REACH * LANES + SIDE * jnp.where(top, row_of - (SIDE - RIM), row_of)
        halo = jnp.where(halo >= REACH * LANES, corner, add_row(halo, row_of))
        index = jnp.concatenate([add_row(straight, row_of), halo], axis=1)
        select = onehot(iota(((REACH + 1) * LANES, 2 * LANES), 0) == index)
        first = 0 if east else SIDE - RIM
        base = 0 if east else REACH
        source = jnp.concatenate(
            [
                jnp.concatenate(
                    [ct_ref[first + i]]
                    + [recv_ref[base + d, i] for d in range(REACH - 1)]
                    + [pltpu.roll(strip_in[3 - east], (LANES - first - i) % LANES, 1)],
                    axis=1,
                )
                for i in range(RIM)
            ],
            axis=0,
        )
        sides = mm(source, select).astype(BF16)
        for i in range(RIM):
            side_ref[east * RIM + i] = sides[C * i : C * (i + 1)]

    for i in range(RIM):
        for east in (0, 1):
            both = side_ref[east * RIM + i]
            fill(east * (RIM + SIDE) + i, both[:, :LANES], both[:, LANES:])

    finish = work((0, 3), True)

    lane_pad = jnp.zeros((HID, 128 - C), F32)
    row_pad = jnp.zeros((PIECE_PAD - PIECE, 128), F32)
    big_ref[...] = jnp.concatenate([acc_ref[1 - core], lane_pad], axis=1).astype(BF16)
    to_core = remote(big_ref, core_in, sum_send.at[0], sum_recv.at[0], partner)
    to_core.start()
    finish(range(1))

    to_core.wait()
    both = jnp.concatenate([acc_ref[core], lane_pad], axis=1) + core_in[...].astype(F32)
    for i in range(PLANE):
        piece = jnp.concatenate([both[PIECE * i : PIECE * (i + 1)], row_pad], axis=0)
        rs_src[i] = piece.astype(BF16)

    def scatter(target, source, at):
        for k in range(1, PLANE):
            i, device = plane_peer(k)
            remote(source(i), target(k), sum_send.at[at], sum_recv.at[at], device).start()

    def settle(ref, count, at):
        block = ref.at[pl.ds(0, count)]
        copy = remote(block, block, sum_send.at[at], sum_recv.at[at], partner)
        copy.wait()

    scatter(lambda k: rs_in.at[k], lambda i: rs_src.at[i], 1)
    finish(range(1, 4))

    totals = [dw_part[g] + gradient(g, (0, 3)) for g in range(GROUPS)]
    totals = jnp.concatenate(totals, axis=0).astype(BF16)
    k_at, n_at = iota((BAND, LANES), 0), iota((BAND, LANES), 1)
    col_at = (k_at % TAPW) // GROUP
    place = onehot((col_at < KS) & (n_at == KS * (k_at // TAPW) + col_at))
    small = mm(totals, place)
    n_at = iota((C, LANES), 1)
    small = jnp.where(n_at == KS * KS, jnp.sum(gg_ref[...], axis=1, keepdims=True), small)
    small = jnp.where(n_at == KS * KS + 1, jnp.sum(gs_ref[...], axis=1, keepdims=True), small)
    small = jnp.concatenate([small[: C // 2, :64], small[C // 2 :, :64]], axis=1).astype(BF16)
    small_plane[me_plane] = small
    scatter(lambda k: small_plane.at[me_plane], lambda i: small_plane.at[me_plane], 3)

    settle(rs_in, PLANE - 1, 1)
    total = rs_src[me_plane].astype(F32)
    for k in range(1, PLANE):
        total = total + rs_in[k].astype(F32)
    y_buf[me_y] = total.astype(BF16)
    for k in range(1, 4):
        remote(y_buf.at[me_y], y_buf.at[me_y], sum_send.at[4], sum_recv.at[4], y_peer(k)).start()

    settle(small_plane, PLANE - 1, 3)
    total = small_plane[0].astype(F32)
    for k in range(1, PLANE):
        total = total + small_plane[k].astype(F32)
    at = 4 * core + me_y
    small_y[at] = total.astype(BF16)
    for device in column_peers:
        remote(small_y.at[at], small_y.at[at], sum_send.at[5], sum_recv.at[5], device).start()

    settle(y_buf, 3, 4)
    total = y_buf[0].astype(F32)
    for k in range(1, 4):
        total = total + y_buf[k].astype(F32)
    ag_buf[core, me_plane] = total.astype(BF16)
    scatter(lambda k: ag_buf.at[core, me_plane], lambda i: ag_buf.at[core, me_plane], 6)

    for w in range(0, SIDE, 4):
        part = jnp.concatenate([ft_ref[w + i] for i in range(4)], axis=0)
        feat_vmem[:, C * w : C * (w + 4)] = jnp.transpose(part)
    store = pltpu.make_async_copy(feat_vmem, feat_ref, local_sem.at[10])
    store.start()

    settle(small_y, 7, 5)
    total = small_y[0].astype(F32)
    for k in range(1, 8):
        total = total + small_y[k].astype(F32)
    small_ref[...] = total
    store_small = pltpu.make_async_copy(small_ref, small_out, local_sem.at[11])
    store_small.start()

    settle(ag_buf.at[core], PLANE - 1, 6)
    last = remote(ag_buf.at[core], ag_buf.at[core], sum_send.at[7], sum_recv.at[7], partner)
    last.start()
    last.wait()
    store_sums = pltpu.make_async_copy(ag_buf, ag_out, local_sem.at[12])
    store_sums.start()
    for copy in (store, store_small, store_sums):
        copy.wait()


def finish_kernel(*refs):
    inputs, outputs, refs = refs[:3], refs[3:9], refs[9:]
    (feat, ag_ref, small_ref), refs = refs[:3], refs[3:]
    (dw_ref, gain_ref, up_ref, down_ref, scale_ref), (sem_in, sem_out) = refs[:5], refs[5:]
    coming = [
        pltpu.make_async_copy(there, here, sem_in.at[i])
        for i, (there, here) in enumerate(zip(inputs, (feat, ag_ref, small_ref)))
    ]
    results = (feat, dw_ref, gain_ref, up_ref, down_ref, scale_ref)
    going = [
        pltpu.make_async_copy(here, there, sem_out.at[i])
        for i, (here, there) in enumerate(zip(results, outputs))
    ]
    for copy in coming:
        copy.start()
    coming[2].wait()
    total = small_ref[...]
    total = jnp.concatenate([total[:, :64], total[:, 64:]], axis=0)
    total = jnp.transpose(jnp.concatenate([total, jnp.zeros((C, 64), F32)], axis=1))
    dw_ref[...] = total[: KS * KS]
    gain_ref[...] = total[KS * KS : KS * KS + 1]
    scale_ref[...] = total[KS * KS + 1 : KS * KS + 2]
    for i in (1, 2, 5):
        going[i].start()
    coming[1].wait()
    for half, ref in ((0, down_ref), (1, up_ref)):
        joined = jnp.concatenate([ag_ref[half, i].astype(F32)[:PIECE] for i in range(PLANE)], axis=0)
        ref[...] = jnp.transpose(joined)[:C]
    for i in (3, 4):
        going[i].start()
    coming[0].wait()
    going[0].start()
    for copy in going:
        copy.wait()


def anywhere(count):
    return [pl.BlockSpec(memory_space=pl.ANY)] * count


def local(
    pixels,
    tissue,
    neighbours,
    upstream,
    stem_weight,
    stem_gain,
    dw_weight,
    norm_gain,
    up_weight,
    down_weight,
    layer_scale,
):
    tiles = lax.axis_size("tile")
    loss_factor = (tiles * lax.axis_size("slab") * SLOTS * SIDE * SIDE) ** (-0.5)
    dma = pltpu.SemaphoreType.DMA
    operands = (
        pixels[0],
        stem_weight,
        stem_gain[None],
        upstream.reshape(LANES, SIDE * C),
        tissue[0],
        dw_weight,
        norm_gain[None],
        up_weight,
        down_weight.T,
        layer_scale[None],
    )
    features, gathered, small = pl.pallas_call(
        functools.partial(whole_kernel, tiles, loss_factor),
        out_shape=(
            jax.ShapeDtypeStruct((LANES, SIDE * C), BF16),
            jax.ShapeDtypeStruct((2, PLANE, PIECE_PAD, 128), BF16),
            jax.ShapeDtypeStruct((C // 2, 128), F32),
        ),
        in_specs=[pl.BlockSpec(memory_space=pltpu.SMEM)] + anywhere(10),
        out_specs=tuple(anywhere(3)),
        scratch_shapes=[pltpu.VMEM(x.shape, x.dtype) for x in operands]
        + [
            pltpu.VMEM((LANES, SIDE * C), BF16),
            pltpu.VMEM((2, PLANE, PIECE_PAD, 128), BF16),
            pltpu.VMEM((C // 2, 128), F32),
            pltpu.VMEM((SIDE, C, LANES), BF16),
            pltpu.VMEM((2, C, LANES), BF16),
            pltpu.VMEM((4, C, LANES), BF16),
            pltpu.VMEM((2 * REACH, RIM, C, LANES), BF16),
            pltpu.VMEM((KS, PADW, C, LANES), BF16),
            pltpu.VMEM((SIDE, C, LANES), BF16),
            pltpu.VMEM((2 * RIM, C, 2 * LANES), BF16),
            pltpu.VMEM((GROUPS, BLOCK * GROUP, BAND), BF16),
            pltpu.VMEM((BLOCK, C, 2 * LANES), F32),
            pltpu.VMEM((BLOCK, C, BLOCKS * LANES), BF16),
            pltpu.VMEM((SIDE, C, LANES), BF16),
            pltpu.VMEM((SIDE, C, LANES), BF16),
            pltpu.VMEM((SIDE, 1, LANES), F32),
            pltpu.VMEM((2, HID, C), F32),
            pltpu.VMEM((C, LANES), F32),
            pltpu.VMEM((C, LANES), F32),
            pltpu.VMEM((HID, 128), BF16),
            pltpu.VMEM((HID, 128), BF16),
            pltpu.VMEM((PLANE, PIECE_PAD, 128), BF16),
            pltpu.VMEM((PLANE, PIECE_PAD, 128), BF16),
            pltpu.VMEM((4, PIECE_PAD, 128), BF16),
            pltpu.VMEM((GROUPS, GROUP, BAND), F32),
            pltpu.VMEM((PLANE, C // 2, 128), BF16),
            pltpu.VMEM((8, C // 2, 128), BF16),
            dma((2 * REACH + 2,)),
            dma((2 * REACH + 2,)),
            dma((8,)),
            dma((8,)),
            dma((13,)),
        ],
        compiler_params=pltpu.CompilerParams(
            collective_id=0, has_side_effects=True, vmem_limit_bytes=VMEM_BYTES
        ),
        name="whole",
    )(neighbours[0], *operands)
    features, grad_dw, grad_gain, grad_up, grad_down_t, grad_scale = pl.pallas_call(
        finish_kernel,
        out_shape=(
            jax.ShapeDtypeStruct((LANES, SIDE * C), BF16),
            jax.ShapeDtypeStruct((KS * KS, C), F32),
            jax.ShapeDtypeStruct((1, C), F32),
            jax.ShapeDtypeStruct((C, HID), F32),
            jax.ShapeDtypeStruct((C, HID), F32),
            jax.ShapeDtypeStruct((1, C), F32),
        ),
        in_specs=anywhere(3),
        out_specs=tuple(anywhere(6)),
        scratch_shapes=[
            pltpu.VMEM((LANES, SIDE * C), BF16),
            pltpu.VMEM((2, PLANE, PIECE_PAD, 128), BF16),
            pltpu.VMEM((C // 2, 128), F32),
            pltpu.VMEM((KS * KS, C), F32),
            pltpu.VMEM((1, C), F32),
            pltpu.VMEM((C, HID), F32),
            pltpu.VMEM((C, HID), F32),
            pltpu.VMEM((1, C), F32),
            dma((3,)),
            dma((6,)),
        ],
        compiler_params=pltpu.CompilerParams(vmem_limit_bytes=VMEM_BYTES),
        name="finish",
    )(features, gathered, small)
    return (
        features.reshape(upstream.shape),
        grad_dw,
        grad_gain[0],
        grad_up,
        grad_down_t.T,
        grad_scale[0],
    )


def solution(mesh):
    placed = (
        P("slab", "tile", None, None),
        P("slab", "tile", None),
        P("slab", "tile", None),
        P("slab", "tile", None, None),
        P(),
        P(),
        P(),
        P(),
        P(),
        P(),
        P(),
    )
    return jax.shard_map(
        local,
        mesh=mesh,
        in_specs=placed,
        out_specs=(P("slab", "tile", None, None), P(), P(), P(), P(), P()),
        check_vma=False,
    )
```

```python
import functools

import jax
import jax.numpy as jnp
from jax import lax
from jax.experimental import pallas as pl
from jax.experimental.pallas import tpu as pltpu
from jax.sharding import PartitionSpec as P

MESH = pl.DeviceIdType.MESH
C = 96
HID = 384
PATCH = 4
KS = 7
SIDE = 32
RIM = 3
REACH = 5
SLOTS = 4
LANES = SLOTS * SIDE
PADW = SIDE + 2 * RIM
GROUP = 16
GROUPS = C // GROUP
BLOCK = 4
BLOCKS = SIDE // BLOCK
TAPW = (BLOCK + RIM * 2) * GROUP
BAND = KS * TAPW
EPS = 1e-06
VMEM_BYTES = 56 * 1024 * 1024
FILL_UNROLL = 32
PLANE = 16
PIECE = HID // PLANE
PIECE_PAD = 32

BF16 = jnp.bfloat16
F32 = jnp.float32


def iota(shape, dim):
    return lax.broadcasted_iota(jnp.int32, shape, dim)


def onehot(mask):
    return jnp.where(mask, 1.0, 0.0).astype(BF16)


def mm(a, b):
    return lax.dot_general(a, b, (((1,), (0,)), ((), ())), preferred_element_type=F32)


def mm_nt(a, b):
    return lax.dot_general(a, b, (((1,), (1,)), ((), ())), preferred_element_type=F32)


def column(row, lanes):
    return jnp.transpose(jnp.broadcast_to(row, (lanes, row.shape[1])))


def gelu_parts(hidden):
    normal_cdf = 0.5 * (1.0 + lax.erf(hidden * 0.7071067811865476))
    density = jnp.exp(-0.5 * hidden * hidden) * 0.3989422804014327
    return (hidden * normal_cdf, normal_cdf + hidden * density)


def remote(source, target, send_sem, recv_sem, device):
    return pltpu.make_async_remote_copy(
        src_ref=source,
        dst_ref=target,
        send_sem=send_sem,
        recv_sem=recv_sem,
        device_id=device,
        device_id_type=MESH,
    )


def whole_kernel(
    tiles,
    loss_factor,
    nb_ref,
    *refs,
):
    inputs, refs = refs[:10], refs[10:]
    (feat_ref, ag_out, small_out), refs = refs[:3], refs[3:]
    held, refs = refs[:10], refs[10:]
    (
        pix_ref,
        stem_ref,
        stem_gain_ref,
        up_vmem,
        tissue_ref,
        dw_ref,
        gain_ref,
        up_ref,
        down_t_ref,
        scale_ref,
    ) = held
    (
        feat_vmem,
        ag_buf,
        small_ref,
        ct_ref,
        strip_ref,
        strip_in,
        recv_ref,
        pt_ref,
        ht_ref,
        side_ref,
        band_ref,
        mixed_ref,
        gm_ref,
        ut_ref,
        ft_ref,
        ts_ref,
        acc_ref,
        gg_ref,
        gs_ref,
        big_ref,
        core_in,
        rs_src,
        rs_in,
        y_buf,
        small_plane,
        small_y,
        send_sem,
        recv_sem,
        sum_send,
        sum_recv,
        gather_recv,
        local_sem,
    ) = refs
    me = lax.axis_index("tile")
    slab = lax.axis_index("slab")
    core = slab % 2
    y_hi = slab // 2
    me_plane = me % PLANE
    y_lo = me // PLANE
    me_y = y_lo + 2 * y_hi

    fetches = [
        pltpu.make_async_copy(there, here, local_sem.at[i])
        for i, (there, here) in enumerate(zip(inputs, held))
    ]
    for copy in fetches:
        copy.start()
    partner = {"tile": me, "slab": 2 * y_hi + (1 - core)}

    def plane_peer(k):
        i = lax.rem(me_plane + k, PLANE)
        return i, {"tile": y_lo * PLANE + i, "slab": slab}

    def y_peer(k, at=core):
        other_lo = lax.rem(y_lo + k % 2, 2)
        other_hi = lax.rem(y_hi + k // 2, 2)
        return {"tile": other_lo * PLANE + me_plane, "slab": 2 * other_hi + at}

    column_peers = [y_peer(k) for k in range(1, 4)] + [y_peer(k, 1 - core) for k in range(4)]

    barrier = pltpu.get_barrier_semaphore()
    greeted = [
        {"tile": lax.rem(me + sign * d + tiles, tiles)} for d in range(1, REACH + 1) for sign in (-1, 1)
    ]
    greeted += [plane_peer(k)[1] for k in range(1, PLANE)]
    greeted += column_peers
    for device in greeted:
        pl.semaphore_signal(barrier, inc=1, device_id=device, device_id_type=MESH)

    for copy in fetches[:3]:
        copy.wait()
    pix = pix_ref[...].reshape(SLOTS * SIDE * PATCH, SIDE * PATCH * 3)
    rows = SLOTS * SIDE * PATCH
    k_at, n_at = iota((rows, rows), 0), iota((rows, rows), 1)
    pick = onehot(k_at == PATCH * (n_at % LANES) + n_at // LANES)
    pix_t = mm(jnp.transpose(pix), pick).astype(BF16)

    q = PATCH * 3
    wt = jnp.transpose(stem_ref[...])
    k_at, n_at = iota((PATCH * q, PATCH * 4 * q), 0), iota((PATCH * q, PATCH * 4 * q), 1)
    spread_q = onehot((k_at // q == n_at // (4 * q)) & (k_at % q == n_at % q))
    wide = mm(wt, spread_q)
    wide = jnp.concatenate([wide] * 4, axis=0)
    r_at, n_at = iota(wide.shape, 0), iota(wide.shape, 1)
    block_w = jnp.where(r_at // C == (n_at % (4 * q)) // q, wide, 0.0).astype(BF16)

    stem_gain = column(stem_gain_ref[...], LANES)
    eight = SIDE // 4
    operand = jnp.concatenate(
        [
            jnp.concatenate(
                [pix_t[4 * q * g : 4 * q * (g + 1), LANES * pr : LANES * (pr + 1)] for pr in range(PATCH)],
                axis=0,
            )
            for g in range(eight)
        ],
        axis=1,
    )
    raw = mm(block_w, operand)
    for v in range(4):
        part = raw[C * v : C * (v + 1)]
        mean = jnp.sum(part, axis=0, keepdims=True) * (1.0 / C)
        part = part - mean
        inverse = lax.rsqrt(jnp.sum(part * part, axis=0, keepdims=True) * (1.0 / C) + EPS)
        part = part * inverse
        for g in range(eight):
            ct_ref[4 * g + v] = (part[:, LANES * g : LANES * (g + 1)] * stem_gain).astype(BF16)

    tiles_here = 0
    for t in range(SLOTS):
        any_side = nb_ref[t, 0]
        for direction in range(1, 8):
            any_side = jnp.maximum(any_side, nb_ref[t, direction])
        tiles_here = tiles_here + jnp.where(any_side >= 0, 1, 0)
    k_at, n_at = iota((LANES, 2 * LANES), 0), iota((LANES, 2 * LANES), 1)
    lower = n_at >= LANES
    kind = (n_at % LANES) // SIDE
    base = onehot(
        (kind < RIM)
        & (k_at // SIDE == jnp.where(lower, tiles_here - 1, 0))
        & (k_at % SIDE == jnp.where(lower, SIDE - RIM + kind, kind))
    )
    col_of = n_at % SIDE
    packed = jnp.zeros((C, 2 * LANES), F32)
    for w in range(0, SIDE, 8):
        left = jnp.concatenate([ct_ref[w + i] for i in range(8)], axis=1)
        right = jnp.concatenate(
            [jnp.where(col_of == w + i, base, jnp.zeros_like(base)) for i in range(8)], axis=0
        )
        packed = packed + mm(left, right)
    for i in range(2):
        strip_ref[i] = packed[:, LANES * i : LANES * (i + 1)].astype(BF16)

    pl.semaphore_wait(barrier, len(greeted))
    strips_sent, sides_sent = [], []
    for d in range(1, REACH + 1):
        back = lax.rem(me - d + tiles, tiles)
        ahead = lax.rem(me + d, tiles)
        if d == 1:
            strips_sent.append((strip_ref.at[0], strip_in.at[0], 10, back))
            strips_sent.append((strip_ref.at[1], strip_in.at[1], 11, ahead))
        if d == REACH:
            sides_sent.append((strip_ref.at[0], strip_in.at[2], d - 1, back))
            sides_sent.append((strip_ref.at[1], strip_in.at[3], REACH + d - 1, ahead))
            continue
        sides_sent.append((ct_ref.at[pl.ds(0, RIM)], recv_ref.at[d - 1], d - 1, back))
        at = REACH + d - 1
        sides_sent.append((ct_ref.at[pl.ds(SIDE - RIM, RIM)], recv_ref.at[at], at, ahead))

    def launch(copies):
        started = []
        for source, target, at, peer in copies:
            copy = remote(source, target, send_sem.at[at], recv_sem.at[at], {"tile": peer})
            copy.start()
            started.append(copy)
        return started

    strips_sent = launch(strips_sent)
    sides_sent = launch(sides_sent)

    for copy in fetches[3:]:
        copy.wait()
    tissue = tissue_ref[...].astype(F32)
    spread_rows = jnp.concatenate(
        [jnp.broadcast_to(tissue[t : t + 1], (SIDE, SIDE * SIDE)) for t in range(SLOTS)], axis=0
    )
    r_at, n_at = iota(spread_rows.shape, 0), iota(spread_rows.shape, 1)
    spread_rows = jnp.where(r_at % SIDE == n_at // SIDE, spread_rows, 0.0).astype(BF16)
    k_at, n_at = iota((SIDE, SIDE * SIDE), 0), iota((SIDE, SIDE * SIDE), 1)
    tissue_t = mm_nt(onehot(k_at == n_at % SIDE), spread_rows)
    for w in range(SIDE):
        ts_ref[w] = tissue_t[w : w + 1]

    for w in range(0, SIDE, 4):
        part = jnp.transpose(up_vmem[:, C * w : C * (w + 4)])
        for i in range(4):
            ut_ref[w + i] = part[C * i : C * (i + 1)]

    taps_t = jnp.transpose(dw_ref[...]).astype(BF16)
    k_at, n_at = iota((KS * KS, BAND), 0), iota((KS * KS, BAND), 1)
    col_at = (n_at % TAPW) // GROUP
    place = onehot((col_at < KS) & (k_at == KS * (n_at // TAPW) + col_at))
    taps = mm(taps_t, place)
    r_at, n_at = iota((GROUP, BAND), 0), iota((GROUP, BAND), 1)
    diagonal = r_at == n_at % GROUP
    for g in range(GROUPS):
        first = jnp.where(diagonal, taps[GROUP * g : GROUP * (g + 1)], 0.0).astype(BF16)
        band_ref[g, :GROUP, :] = first
        for w in range(1, BLOCK):
            band_ref[g, GROUP * w : GROUP * (w + 1), :] = pltpu.roll(first, GROUP * w, 1)

    lane = iota((1, LANES), 1)
    slot_of, row_of = lane // SIDE, lane % SIDE

    def per_tile(direction, rule):
        out = []
        for t in range(SLOTS):
            n = nb_ref[t, direction]
            out.append(jnp.where(n >= 0, rule(jnp.maximum(n, 0)), -1))
        return out

    def spread(values, shift):
        result = jnp.full((1, LANES), -1, jnp.int32)
        for t in range(SLOTS):
            result = jnp.where(slot_of == (t + shift) % SLOTS, values[t], result)
        return result

    def add_row(index, row):
        return jnp.where(index >= 0, index + row, -1)

    top = row_of >= SIDE - RIM
    bottom = row_of < RIM

    def own_rule(n):
        return jnp.where(n // SLOTS == me, (n % SLOTS) * SIDE, -1)

    def other_rule(n):
        return jnp.where(n // SLOTS == me, -1, 1)

    own_above = spread(per_tile(0, own_rule), -1)
    own_below = spread(per_tile(1, own_rule), 1)
    own = add_row(jnp.where(top, own_above, jnp.where(bottom, own_below, -1)), row_of)
    select_own = onehot(iota((LANES, LANES), 0) == own)
    for w in range(0, SIDE, 8):
        near = mm(jnp.concatenate([ct_ref[w + i] for i in range(8)], axis=0), select_own).astype(BF16)
        for i in range(8):
            ht_ref[w + i] = near[C * i : C * (i + 1)]

    far_above = spread(per_tile(0, other_rule), -1)
    far_below = spread(per_tile(1, other_rule), 1)
    far = jnp.where(
        top & (far_above >= 0),
        row_of - (SIDE - RIM),
        jnp.where(bottom & (far_below >= 0), SLOTS + row_of, -1),
    )
    k_at = iota((2 * LANES, LANES), 0)
    far_base = onehot(k_at // SIDE == far)
    col_of = k_at % SIDE

    up_w = up_ref[...]
    down_t = down_t_ref[...]
    up_t = jnp.transpose(up_w)
    down_w = jnp.transpose(down_t)
    gain = column(gain_ref[...], LANES)
    scale = column(scale_ref[...], LANES)
    gain = jnp.concatenate([gain] * 4, axis=1)
    scale = jnp.concatenate([scale] * 4, axis=1)
    acc_ref[...] = jnp.zeros_like(acc_ref)
    gg_ref[...] = jnp.zeros_like(gg_ref)
    gs_ref[...] = jnp.zeros_like(gs_ref)

    for copy in strips_sent:
        copy.wait()
    strips = jnp.concatenate([strip_in[1], strip_in[0]], axis=1)
    for w in range(0, SIDE, 4):
        select_far = jnp.concatenate(
            [jnp.where(col_of == w + i, far_base, jnp.zeros_like(far_base)) for i in range(4)], axis=1
        )
        got = mm(strips, select_far).astype(BF16)
        for i in range(4):
            ht_ref[w + i] = ht_ref[w + i] + got[:, LANES * i : LANES * (i + 1)]

    def fill(at, centre, halo):
        for a in range(KS):
            s = a - RIM
            if s > 0:
                value = pltpu.roll(jnp.where(row_of < s, halo, centre), LANES - s, 1)
            elif s < 0:
                value = pltpu.roll(jnp.where(row_of >= SIDE + s, halo, centre), -s, 1)
            else:
                value = centre
            pt_ref[a, at] = value

    def fill_step(w, carry):
        fill(RIM + w, ct_ref[w], ht_ref[w])
        return carry

    lax.fori_loop(0, SIDE, fill_step, 0, unroll=FILL_UNROLL)

    def window(g, blocks):
        return jnp.concatenate(
            [
                jnp.concatenate(
                    [
                        pt_ref[a, BLOCK * j : BLOCK * j + TAPW // GROUP, GROUP * g : GROUP * (g + 1)].reshape(
                            TAPW, LANES
                        )
                        for a in range(KS)
                    ],
                    axis=0,
                )
                for j in blocks
            ],
            axis=1,
        )

    def fold(values):
        total = values[:, :LANES]
        for j in range(1, values.shape[1] // LANES):
            total = total + values[:, LANES * j : LANES * (j + 1)]
        return total

    def work(blocks, defer):
        for g in range(GROUPS):
            out = mm(band_ref[g], window(g, blocks))
            for w in range(BLOCK):
                mixed_ref[w, GROUP * g : GROUP * (g + 1), : out.shape[1]] = out[GROUP * w : GROUP * (w + 1)]

        columns = [(w, j) for w in range(BLOCK) for j in blocks]
        steps = len(columns) // 4

        def pair_of(i):
            return columns[4 * i : 4 * (i + 1)]

        def gather(ref, i):
            return jnp.concatenate([ref[BLOCK * j + w] for w, j in pair_of(i)], axis=1)

        def front(i):
            tissue = gather(ts_ref, i)
            grad_out = gather(ut_ref, i).astype(F32) * (tissue * loss_factor)
            grad_branch = (grad_out * scale).astype(BF16)
            grad_active = mm(down_w, grad_branch)
            places = [(w, LANES * blocks.index(j)) for w, j in pair_of(i)]
            mixed = jnp.concatenate([mixed_ref[w, :, at : at + LANES] for w, at in places], axis=1)
            mean = jnp.sum(mixed, axis=0, keepdims=True) * (1.0 / C)
            centered = mixed - mean
            inverse = lax.rsqrt(jnp.sum(centered * centered, axis=0, keepdims=True) * (1.0 / C) + EPS)
            normed = centered * inverse
            lowered = (normed * gain).astype(BF16)
            hidden = mm(up_t, lowered)
            return tissue, grad_out, grad_branch, grad_active, normed, inverse, lowered, hidden

        def middle(state):
            grad_active, hidden = state[3], state[7]
            active, steepness = gelu_parts(hidden)
            return active.astype(BF16), (grad_active * steepness).astype(BF16)

        def large(state, pair):
            active, grad_hidden = pair
            acc_ref[0] += mm_nt(active, state[2])
            acc_ref[1] += mm_nt(grad_hidden, state[6])

        def back(i, state, pair):
            tissue, grad_out, _, _, normed, inverse, _, _ = state
            active, grad_hidden = pair
            grad_lowered = mm(up_w, grad_hidden)
            branch = mm(down_t, active)
            summed = gather(ct_ref, i).astype(F32) + scale * branch
            features = (summed * tissue).astype(BF16)
            gs_ref[...] += fold(grad_out * branch)
            gg_ref[...] += fold(grad_lowered * normed)
            scaled = grad_lowered * gain
            mean_one = jnp.sum(scaled, axis=0, keepdims=True) * (1.0 / C)
            mean_two = jnp.sum(scaled * normed, axis=0, keepdims=True) * (1.0 / C)
            grad_mixed = (inverse * (scaled - mean_one - normed * mean_two)).astype(BF16)
            for at, (w, j) in enumerate(pair_of(i)):
                lanes = slice(LANES * at, LANES * (at + 1))
                gm_ref[w, :, LANES * j : LANES * (j + 1)] = grad_mixed[:, lanes]
                ft_ref[BLOCK * j + w] = features[:, lanes]

        kept = []
        state = front(0)
        for i in range(steps):
            pair = middle(state)
            later = front(i + 1) if i + 1 < steps else None
            large(state, pair)
            if defer:
                kept.append((i, state, pair))
            else:
                back(i, state, pair)
            state = later

        def finish(some):
            for i in some:
                back(*kept[i])

        return finish

    work(tuple(range(1, BLOCKS - 1)), False)

    def gradient(g, blocks):
        left = jnp.concatenate(
            [
                jnp.concatenate(
                    [gm_ref[w, GROUP * g : GROUP * (g + 1), LANES * j : LANES * (j + 1)] for j in blocks],
                    axis=1,
                )
                for w in range(BLOCK)
            ],
            axis=0,
        )
        full = mm_nt(left, window(g, blocks))
        total = None
        for w in range(BLOCK):
            part = jnp.where(diagonal, full[GROUP * w : GROUP * (w + 1)], 0.0)
            if w:
                part = pltpu.roll(part, BAND - GROUP * w, 1)
            total = part if total is None else total + part
        return total


    for copy in sides_sent:
        copy.wait()
    for east in (0, 1):
        def rule(n, east=east):
            away = n // SLOTS - me
            away = away if east else -away
            return away * LANES + (n % SLOTS) * SIDE

        straight = spread(per_tile(2 + east, rule), 0)
        above = spread(per_tile(4 + east, rule), -1)
        below = spread(per_tile(6 + east, rule), 1)
        halo = jnp.where(top, above, jnp.where(bottom, below, -1))
        corner = REACH * LANES + SIDE * jnp.where(top, row_of - (SIDE - RIM), row_of)
        halo = jnp.where(halo >= REACH * LANES, corner, add_row(halo, row_of))
        index = jnp.concatenate([add_row(straight, row_of), halo], axis=1)
        select = onehot(iota(((REACH + 1) * LANES, 2 * LANES), 0) == index)
        first = 0 if east else SIDE - RIM
        base = 0 if east else REACH
        source = jnp.concatenate(
            [
                jnp.concatenate(
                    [ct_ref[first + i]]
                    + [recv_ref[base + d, i] for d in range(REACH - 1)]
                    + [pltpu.roll(strip_in[3 - east], (LANES - first - i) % LANES, 1)],
                    axis=1,
                )
                for i in range(RIM)
            ],
            axis=0,
        )
        sides = mm(source, select).astype(BF16)
        for i in range(RIM):
            side_ref[east * RIM + i] = sides[C * i : C * (i + 1)]

    for i in range(RIM):
        for east in (0, 1):
            both = side_ref[east * RIM + i]
            fill(east * (RIM + SIDE) + i, both[:, :LANES], both[:, LANES:])

    finish = work((0, BLOCKS - 1), True)

    lane_pad = jnp.zeros((HID, 128 - C), F32)
    row_pad = jnp.zeros((PIECE_PAD - PIECE, 128), F32)
    big_ref[...] = jnp.concatenate([acc_ref[1 - core], lane_pad], axis=1).astype(BF16)
    to_core = remote(big_ref, core_in, sum_send.at[0], sum_recv.at[0], partner)
    to_core.start()
    finish(range(1))

    to_core.wait()
    both = jnp.concatenate([acc_ref[core], lane_pad], axis=1) + core_in[...].astype(F32)
    for i in range(PLANE):
        piece = jnp.concatenate([both[PIECE * i : PIECE * (i + 1)], row_pad], axis=0)
        rs_src[i] = piece.astype(BF16)

    def scatter(target, source, at):
        for k in range(1, PLANE):
            i, device = plane_peer(k)
            remote(source(i), target(k), sum_send.at[at], sum_recv.at[at], device).start()

    def settle(ref, count, at):
        block = ref.at[pl.ds(0, count)]
        copy = remote(block, block, sum_send.at[at], sum_recv.at[at], partner)
        copy.wait()

    scatter(lambda k: rs_in.at[k], lambda i: rs_src.at[i], 1)
    finish(range(1, 2))

    totals = [gradient(g, range(BLOCKS)) for g in range(GROUPS)]
    totals = jnp.concatenate(totals, axis=0).astype(BF16)
    k_at, n_at = iota((BAND, LANES), 0), iota((BAND, LANES), 1)
    col_at = (k_at % TAPW) // GROUP
    place = onehot((col_at < KS) & (n_at == KS * (k_at // TAPW) + col_at))
    small = mm(totals, place)
    n_at = iota((C, LANES), 1)
    small = jnp.where(n_at == KS * KS, jnp.sum(gg_ref[...], axis=1, keepdims=True), small)
    small = jnp.where(n_at == KS * KS + 1, jnp.sum(gs_ref[...], axis=1, keepdims=True), small)
    small = jnp.concatenate([small[: C // 2, :64], small[C // 2 :, :64]], axis=1).astype(BF16)
    small_plane[me_plane] = small
    scatter(lambda k: small_plane.at[me_plane], lambda i: small_plane.at[me_plane], 3)

    settle(rs_in, PLANE - 1, 1)
    total = rs_src[me_plane].astype(F32)
    for k in range(1, PLANE):
        total = total + rs_in[k].astype(F32)
    y_buf[me_y] = total.astype(BF16)
    for k in range(1, 4):
        remote(y_buf.at[me_y], y_buf.at[me_y], sum_send.at[4], sum_recv.at[4], y_peer(k)).start()

    settle(small_plane, PLANE - 1, 3)
    total = small_plane[0].astype(F32)
    for k in range(1, PLANE):
        total = total + small_plane[k].astype(F32)
    at = 4 * core + me_y
    small_y[at] = total.astype(BF16)
    for device in column_peers:
        remote(small_y.at[at], small_y.at[at], sum_send.at[5], sum_recv.at[5], device).start()

    settle(y_buf, 3, 4)
    total = y_buf[0].astype(F32)
    for k in range(1, 4):
        total = total + y_buf[k].astype(F32)
    ag_buf[core, me_plane] = total.astype(BF16)
    mine = ag_buf.at[core, me_plane]
    for k in range(1, PLANE):
        remote(mine, mine, sum_send.at[6], gather_recv.at[k], plane_peer(k)[1]).start()
    remote(mine, mine, sum_send.at[7], sum_recv.at[7], partner).start()

    for w in range(0, SIDE, 4):
        part = jnp.concatenate([ft_ref[w + i] for i in range(4)], axis=0)
        feat_vmem[:, C * w : C * (w + 4)] = jnp.transpose(part)
    store = pltpu.make_async_copy(feat_vmem, feat_ref, local_sem.at[10])
    store.start()

    settle(small_y, 7, 5)
    total = small_y[0].astype(F32)
    for k in range(1, 8):
        total = total + small_y[k].astype(F32)
    small_ref[...] = total
    store_small = pltpu.make_async_copy(small_ref, small_out, local_sem.at[11])
    store_small.start()

    for k in range(1, PLANE):
        piece = ag_buf.at[core, lax.rem(me_plane + PLANE - k, PLANE)]
        remote(piece, piece, sum_send.at[6], gather_recv.at[k], partner).wait_recv()
        remote(piece, piece, sum_send.at[7], sum_recv.at[7], partner).start()
    sent = ag_buf.at[core, pl.ds(0, PLANE - 1)]
    remote(sent, sent, sum_send.at[6], sum_recv.at[6], partner).wait_send()
    other = ag_buf.at[1 - core]
    remote(other, other, sum_send.at[7], sum_recv.at[7], partner).wait()
    store_sums = pltpu.make_async_copy(ag_buf, ag_out, local_sem.at[12])
    store_sums.start()
    for copy in (store, store_small, store_sums):
        copy.wait()


def finish_kernel(*refs):
    inputs, outputs, refs = refs[:3], refs[3:9], refs[9:]
    (feat, ag_ref, small_ref), refs = refs[:3], refs[3:]
    (dw_ref, gain_ref, up_ref, down_ref, scale_ref), (sem_in, sem_out) = refs[:5], refs[5:]
    coming = [
        pltpu.make_async_copy(there, here, sem_in.at[i])
        for i, (there, here) in enumerate(zip(inputs, (feat, ag_ref, small_ref)))
    ]
    results = (feat, dw_ref, gain_ref, up_ref, down_ref, scale_ref)
    going = [
        pltpu.make_async_copy(here, there, sem_out.at[i])
        for i, (here, there) in enumerate(zip(results, outputs))
    ]
    for copy in coming:
        copy.start()
    coming[0].wait()
    going[0].start()
    coming[2].wait()
    total = small_ref[...]
    total = jnp.concatenate([total[:, :64], total[:, 64:]], axis=0)
    total = jnp.transpose(jnp.concatenate([total, jnp.zeros((C, 64), F32)], axis=1))
    dw_ref[...] = total[: KS * KS]
    gain_ref[...] = total[KS * KS : KS * KS + 1]
    scale_ref[...] = total[KS * KS + 1 : KS * KS + 2]
    for i in (1, 2, 5):
        going[i].start()
    coming[1].wait()
    for half, ref in ((0, down_ref), (1, up_ref)):
        joined = jnp.concatenate([ag_ref[half, i].astype(F32)[:PIECE] for i in range(PLANE)], axis=0)
        ref[...] = jnp.transpose(joined)[:C]
    for i in (3, 4):
        going[i].start()
    for copy in going:
        copy.wait()


def anywhere(count):
    return [pl.BlockSpec(memory_space=pl.ANY)] * count


def local(
    pixels,
    tissue,
    neighbours,
    upstream,
    stem_weight,
    stem_gain,
    dw_weight,
    norm_gain,
    up_weight,
    down_weight,
    layer_scale,
):
    tiles = lax.axis_size("tile")
    loss_factor = (tiles * lax.axis_size("slab") * SLOTS * SIDE * SIDE) ** (-0.5)
    dma = pltpu.SemaphoreType.DMA
    operands = (
        pixels[0],
        stem_weight,
        stem_gain[None],
        upstream.reshape(LANES, SIDE * C),
        tissue[0],
        dw_weight,
        norm_gain[None],
        up_weight,
        down_weight.T,
        layer_scale[None],
    )
    features, gathered, small = pl.pallas_call(
        functools.partial(whole_kernel, tiles, loss_factor),
        out_shape=(
            jax.ShapeDtypeStruct((LANES, SIDE * C), BF16),
            jax.ShapeDtypeStruct((2, PLANE, PIECE_PAD, 128), BF16),
            jax.ShapeDtypeStruct((C // 2, 128), F32),
        ),
        in_specs=[pl.BlockSpec(memory_space=pltpu.SMEM)] + anywhere(10),
        out_specs=tuple(anywhere(3)),
        scratch_shapes=[pltpu.VMEM(x.shape, x.dtype) for x in operands]
        + [
            pltpu.VMEM((LANES, SIDE * C), BF16),
            pltpu.VMEM((2, PLANE, PIECE_PAD, 128), BF16),
            pltpu.VMEM((C // 2, 128), F32),
            pltpu.VMEM((SIDE, C, LANES), BF16),
            pltpu.VMEM((2, C, LANES), BF16),
            pltpu.VMEM((4, C, LANES), BF16),
            pltpu.VMEM((2 * REACH, RIM, C, LANES), BF16),
            pltpu.VMEM((KS, PADW, C, LANES), BF16),
            pltpu.VMEM((SIDE, C, LANES), BF16),
            pltpu.VMEM((2 * RIM, C, 2 * LANES), BF16),
            pltpu.VMEM((GROUPS, BLOCK * GROUP, BAND), BF16),
            pltpu.VMEM((BLOCK, C, (BLOCKS - 2) * LANES), F32),
            pltpu.VMEM((BLOCK, C, BLOCKS * LANES), BF16),
            pltpu.VMEM((SIDE, C, LANES), BF16),
            pltpu.VMEM((SIDE, C, LANES), BF16),
            pltpu.VMEM((SIDE, 1, LANES), F32),
            pltpu.VMEM((2, HID, C), F32),
            pltpu.VMEM((C, LANES), F32),
            pltpu.VMEM((C, LANES), F32),
            pltpu.VMEM((HID, 128), BF16),
            pltpu.VMEM((HID, 128), BF16),
            pltpu.VMEM((PLANE, PIECE_PAD, 128), BF16),
            pltpu.VMEM((PLANE, PIECE_PAD, 128), BF16),
            pltpu.VMEM((4, PIECE_PAD, 128), BF16),
            pltpu.VMEM((PLANE, C // 2, 128), BF16),
            pltpu.VMEM((8, C // 2, 128), BF16),
            dma((2 * REACH + 2,)),
            dma((2 * REACH + 2,)),
            dma((8,)),
            dma((8,)),
            dma((PLANE,)),
            dma((13,)),
        ],
        compiler_params=pltpu.CompilerParams(
            collective_id=0, has_side_effects=True, vmem_limit_bytes=VMEM_BYTES
        ),
        name="whole",
    )(neighbours[0], *operands)
    features, grad_dw, grad_gain, grad_up, grad_down_t, grad_scale = pl.pallas_call(
        finish_kernel,
        out_shape=(
            jax.ShapeDtypeStruct((LANES, SIDE * C), BF16),
            jax.ShapeDtypeStruct((KS * KS, C), F32),
            jax.ShapeDtypeStruct((1, C), F32),
            jax.ShapeDtypeStruct((C, HID), F32),
            jax.ShapeDtypeStruct((C, HID), F32),
            jax.ShapeDtypeStruct((1, C), F32),
        ),
        in_specs=anywhere(3),
        out_specs=tuple(anywhere(6)),
        scratch_shapes=[
            pltpu.VMEM((LANES, SIDE * C), BF16),
            pltpu.VMEM((2, PLANE, PIECE_PAD, 128), BF16),
            pltpu.VMEM((C // 2, 128), F32),
            pltpu.VMEM((KS * KS, C), F32),
            pltpu.VMEM((1, C), F32),
            pltpu.VMEM((C, HID), F32),
            pltpu.VMEM((C, HID), F32),
            pltpu.VMEM((1, C), F32),
            dma((3,)),
            dma((6,)),
        ],
        compiler_params=pltpu.CompilerParams(vmem_limit_bytes=VMEM_BYTES),
        name="finish",
    )(features, gathered, small)
    return (
        features.reshape(upstream.shape),
        grad_dw,
        grad_gain[0],
        grad_up,
        grad_down_t.T,
        grad_scale[0],
    )


def solution(mesh):
    placed = (
        P("slab", "tile", None, None),
        P("slab", "tile", None),
        P("slab", "tile", None),
        P("slab", "tile", None, None),
        P(),
        P(),
        P(),
        P(),
        P(),
        P(),
        P(),
    )
    return jax.shard_map(
        local,
        mesh=mesh,
        in_specs=placed,
        out_specs=(P("slab", "tile", None, None), P(), P(), P(), P(), P()),
        check_vma=False,
    )
```

```python
import functools

import jax
import jax.numpy as jnp
from jax import lax
from jax.experimental import pallas as pl
from jax.experimental.pallas import tpu as pltpu
from jax.sharding import PartitionSpec as P

MESH = pl.DeviceIdType.MESH
C = 96
HID = 384
PATCH = 4
KS = 7
SIDE = 32
RIM = 3
REACH = 5
SLOTS = 4
LANES = SLOTS * SIDE
PADW = SIDE + 2 * RIM
GROUP = 16
GROUPS = C // GROUP
BLOCK = 4
BLOCKS = SIDE // BLOCK
TAPW = (BLOCK + RIM * 2) * GROUP
BAND = KS * TAPW
EPS = 1e-06
VMEM_BYTES = 56 * 1024 * 1024
FILL_UNROLL = 32
PLANE = 16
PIECE = HID // PLANE
PIECE_PAD = 32

BF16 = jnp.bfloat16
F32 = jnp.float32


def iota(shape, dim):
    return lax.broadcasted_iota(jnp.int32, shape, dim)


def onehot(mask):
    return jnp.where(mask, 1.0, 0.0).astype(BF16)


def mm(a, b):
    return lax.dot_general(a, b, (((1,), (0,)), ((), ())), preferred_element_type=F32)


def mm_nt(a, b):
    return lax.dot_general(a, b, (((1,), (1,)), ((), ())), preferred_element_type=F32)


def column(row, lanes):
    return jnp.transpose(jnp.broadcast_to(row, (lanes, row.shape[1])))


def gelu_parts(hidden):
    normal_cdf = 0.5 * (1.0 + lax.erf(hidden * 0.7071067811865476))
    density = jnp.exp(-0.5 * hidden * hidden) * 0.3989422804014327
    return (hidden * normal_cdf, normal_cdf + hidden * density)


def remote(source, target, send_sem, recv_sem, device):
    return pltpu.make_async_remote_copy(
        src_ref=source,
        dst_ref=target,
        send_sem=send_sem,
        recv_sem=recv_sem,
        device_id=device,
        device_id_type=MESH,
    )


def whole_kernel(
    tiles,
    loss_factor,
    nb_ref,
    *refs,
):
    inputs, refs = refs[:10], refs[10:]
    (feat_ref, ag_out, small_out), refs = refs[:3], refs[3:]
    held, refs = refs[:10], refs[10:]
    (
        pix_ref,
        stem_ref,
        stem_gain_ref,
        up_vmem,
        tissue_ref,
        dw_ref,
        gain_ref,
        up_ref,
        down_t_ref,
        scale_ref,
    ) = held
    (
        feat_vmem,
        ag_buf,
        small_ref,
        ct_ref,
        strip_ref,
        strip_in,
        recv_ref,
        pt_ref,
        ht_ref,
        side_ref,
        band_ref,
        mixed_ref,
        gm_ref,
        ut_ref,
        ft_ref,
        ts_ref,
        acc_ref,
        gg_ref,
        gs_ref,
        big_ref,
        core_in,
        rs_src,
        rs_in,
        y_buf,
        small_plane,
        small_y,
        send_sem,
        recv_sem,
        sum_send,
        sum_recv,
        gather_recv,
        local_sem,
    ) = refs
    me = lax.axis_index("tile")
    slab = lax.axis_index("slab")
    core = slab % 2
    y_hi = slab // 2
    me_plane = me % PLANE
    y_lo = me // PLANE
    me_y = y_lo + 2 * y_hi

    fetches = [
        pltpu.make_async_copy(there, here, local_sem.at[i])
        for i, (there, here) in enumerate(zip(inputs, held))
    ]
    for copy in fetches:
        copy.start()
    partner = {"tile": me, "slab": 2 * y_hi + (1 - core)}

    def plane_peer(k):
        i = lax.rem(me_plane + k, PLANE)
        return i, {"tile": y_lo * PLANE + i, "slab": slab}

    def y_peer(k, at=core):
        other_lo = lax.rem(y_lo + k % 2, 2)
        other_hi = lax.rem(y_hi + k // 2, 2)
        return {"tile": other_lo * PLANE + me_plane, "slab": 2 * other_hi + at}

    column_peers = [y_peer(k) for k in range(1, 4)] + [y_peer(k, 1 - core) for k in range(4)]

    barrier = pltpu.get_barrier_semaphore()
    greeted = [
        {"tile": lax.rem(me + sign * d + tiles, tiles)} for d in range(1, REACH + 1) for sign in (-1, 1)
    ]
    greeted += [plane_peer(k)[1] for k in range(1, PLANE)]
    greeted += column_peers
    for device in greeted:
        pl.semaphore_signal(barrier, inc=1, device_id=device, device_id_type=MESH)

    for copy in fetches[:3]:
        copy.wait()
    pix = pix_ref[...].reshape(SLOTS * SIDE * PATCH, SIDE * PATCH * 3)
    rows = SLOTS * SIDE * PATCH
    k_at, n_at = iota((rows, rows), 0), iota((rows, rows), 1)
    pick = onehot(k_at == PATCH * (n_at % LANES) + n_at // LANES)
    pix_t = mm(jnp.transpose(pix), pick).astype(BF16)

    q = PATCH * 3
    wt = jnp.transpose(stem_ref[...])
    k_at, n_at = iota((PATCH * q, PATCH * 4 * q), 0), iota((PATCH * q, PATCH * 4 * q), 1)
    spread_q = onehot((k_at // q == n_at // (4 * q)) & (k_at % q == n_at % q))
    wide = mm(wt, spread_q)
    wide = jnp.concatenate([wide] * 4, axis=0)
    r_at, n_at = iota(wide.shape, 0), iota(wide.shape, 1)
    block_w = jnp.where(r_at // C == (n_at % (4 * q)) // q, wide, 0.0).astype(BF16)

    stem_gain = column(stem_gain_ref[...], LANES)
    eight = SIDE // 4
    operand = jnp.concatenate(
        [
            jnp.concatenate(
                [pix_t[4 * q * g : 4 * q * (g + 1), LANES * pr : LANES * (pr + 1)] for pr in range(PATCH)],
                axis=0,
            )
            for g in range(eight)
        ],
        axis=1,
    )
    raw = mm(block_w, operand)
    for v in range(4):
        part = raw[C * v : C * (v + 1)]
        mean = jnp.sum(part, axis=0, keepdims=True) * (1.0 / C)
        part = part - mean
        inverse = lax.rsqrt(jnp.sum(part * part, axis=0, keepdims=True) * (1.0 / C) + EPS)
        part = part * inverse
        for g in range(eight):
            ct_ref[4 * g + v] = (part[:, LANES * g : LANES * (g + 1)] * stem_gain).astype(BF16)

    tiles_here = 0
    for t in range(SLOTS):
        any_side = nb_ref[t, 0]
        for direction in range(1, 8):
            any_side = jnp.maximum(any_side, nb_ref[t, direction])
        tiles_here = tiles_here + jnp.where(any_side >= 0, 1, 0)
    k_at, n_at = iota((LANES, 2 * LANES), 0), iota((LANES, 2 * LANES), 1)
    lower = n_at >= LANES
    kind = (n_at % LANES) // SIDE
    base = onehot(
        (kind < RIM)
        & (k_at // SIDE == jnp.where(lower, tiles_here - 1, 0))
        & (k_at % SIDE == jnp.where(lower, SIDE - RIM + kind, kind))
    )
    col_of = n_at % SIDE
    packed = jnp.zeros((C, 2 * LANES), F32)
    for w in range(0, SIDE, 8):
        left = jnp.concatenate([ct_ref[w + i] for i in range(8)], axis=1)
        right = jnp.concatenate(
            [jnp.where(col_of == w + i, base, jnp.zeros_like(base)) for i in range(8)], axis=0
        )
        packed = packed + mm(left, right)
    for i in range(2):
        strip_ref[i] = packed[:, LANES * i : LANES * (i + 1)].astype(BF16)

    pl.semaphore_wait(barrier, len(greeted))
    strips_sent, sides_sent = [], []
    for d in range(1, REACH + 1):
        back = lax.rem(me - d + tiles, tiles)
        ahead = lax.rem(me + d, tiles)
        if d == 1:
            strips_sent.append((strip_ref.at[0], strip_in.at[0], 10, back))
            strips_sent.append((strip_ref.at[1], strip_in.at[1], 11, ahead))
        if d == REACH:
            sides_sent.append((strip_ref.at[0], strip_in.at[2], d - 1, back))
            sides_sent.append((strip_ref.at[1], strip_in.at[3], REACH + d - 1, ahead))
            continue
        sides_sent.append((ct_ref.at[pl.ds(0, RIM)], recv_ref.at[d - 1], d - 1, back))
        at = REACH + d - 1
        sides_sent.append((ct_ref.at[pl.ds(SIDE - RIM, RIM)], recv_ref.at[at], at, ahead))

    def launch(copies):
        started = []
        for source, target, at, peer in copies:
            copy = remote(source, target, send_sem.at[at], recv_sem.at[at], {"tile": peer})
            copy.start()
            started.append(copy)
        return started

    strips_sent = launch(strips_sent)
    sides_sent = launch([sides_sent[i] for i in (0, 1, 6, 7, 4, 5, 2, 3, 8, 9)])

    for copy in fetches[3:]:
        copy.wait()
    tissue = tissue_ref[...].astype(F32)
    spread_rows = jnp.concatenate(
        [jnp.broadcast_to(tissue[t : t + 1], (SIDE, SIDE * SIDE)) for t in range(SLOTS)], axis=0
    )
    r_at, n_at = iota(spread_rows.shape, 0), iota(spread_rows.shape, 1)
    spread_rows = jnp.where(r_at % SIDE == n_at // SIDE, spread_rows, 0.0).astype(BF16)
    k_at, n_at = iota((SIDE, SIDE * SIDE), 0), iota((SIDE, SIDE * SIDE), 1)
    tissue_t = mm_nt(onehot(k_at == n_at % SIDE), spread_rows)
    for w in range(SIDE):
        ts_ref[w] = tissue_t[w : w + 1]

    for w in range(0, SIDE, 4):
        part = jnp.transpose(up_vmem[:, C * w : C * (w + 4)])
        for i in range(4):
            ut_ref[w + i] = part[C * i : C * (i + 1)]

    taps_t = jnp.transpose(dw_ref[...]).astype(BF16)
    k_at, n_at = iota((KS * KS, BAND), 0), iota((KS * KS, BAND), 1)
    col_at = (n_at % TAPW) // GROUP
    place = onehot((col_at < KS) & (k_at == KS * (n_at // TAPW) + col_at))
    taps = mm(taps_t, place)
    r_at, n_at = iota((GROUP, BAND), 0), iota((GROUP, BAND), 1)
    diagonal = r_at == n_at % GROUP
    for g in range(GROUPS):
        first = jnp.where(diagonal, taps[GROUP * g : GROUP * (g + 1)], 0.0).astype(BF16)
        band_ref[g, :GROUP, :] = first
        for w in range(1, BLOCK):
            band_ref[g, GROUP * w : GROUP * (w + 1), :] = pltpu.roll(first, GROUP * w, 1)

    lane = iota((1, LANES), 1)
    slot_of, row_of = lane // SIDE, lane % SIDE

    def per_tile(direction, rule):
        out = []
        for t in range(SLOTS):
            n = nb_ref[t, direction]
            out.append(jnp.where(n >= 0, rule(jnp.maximum(n, 0)), -1))
        return out

    def spread(values, shift):
        result = jnp.full((1, LANES), -1, jnp.int32)
        for t in range(SLOTS):
            result = jnp.where(slot_of == (t + shift) % SLOTS, values[t], result)
        return result

    def add_row(index, row):
        return jnp.where(index >= 0, index + row, -1)

    top = row_of >= SIDE - RIM
    bottom = row_of < RIM

    def own_rule(n):
        return jnp.where(n // SLOTS == me, (n % SLOTS) * SIDE, -1)

    def other_rule(n):
        return jnp.where(n // SLOTS == me, -1, 1)

    own_above = spread(per_tile(0, own_rule), -1)
    own_below = spread(per_tile(1, own_rule), 1)
    own = add_row(jnp.where(top, own_above, jnp.where(bottom, own_below, -1)), row_of)
    select_own = onehot(iota((LANES, LANES), 0) == own)
    for w in range(0, SIDE, 8):
        near = mm(jnp.concatenate([ct_ref[w + i] for i in range(8)], axis=0), select_own).astype(BF16)
        for i in range(8):
            ht_ref[w + i] = near[C * i : C * (i + 1)]

    far_above = spread(per_tile(0, other_rule), -1)
    far_below = spread(per_tile(1, other_rule), 1)
    far = jnp.where(
        top & (far_above >= 0),
        row_of - (SIDE - RIM),
        jnp.where(bottom & (far_below >= 0), SLOTS + row_of, -1),
    )
    k_at = iota((2 * LANES, LANES), 0)
    far_base = onehot(k_at // SIDE == far)
    col_of = k_at % SIDE

    up_w = up_ref[...]
    down_t = down_t_ref[...]
    up_t = jnp.transpose(up_w)
    down_w = jnp.transpose(down_t)
    gain = column(gain_ref[...], LANES)
    scale = column(scale_ref[...], LANES)
    gain = jnp.concatenate([gain] * 4, axis=1)
    scale = jnp.concatenate([scale] * 4, axis=1)
    acc_ref[...] = jnp.zeros_like(acc_ref)
    gg_ref[...] = jnp.zeros_like(gg_ref)
    gs_ref[...] = jnp.zeros_like(gs_ref)

    for copy in strips_sent:
        copy.wait()
    strips = jnp.concatenate([strip_in[1], strip_in[0]], axis=1)
    for w in range(0, SIDE, 4):
        select_far = jnp.concatenate(
            [jnp.where(col_of == w + i, far_base, jnp.zeros_like(far_base)) for i in range(4)], axis=1
        )
        got = mm(strips, select_far).astype(BF16)
        for i in range(4):
            ht_ref[w + i] = ht_ref[w + i] + got[:, LANES * i : LANES * (i + 1)]

    def fill(at, centre, halo):
        for a in range(KS):
            s = a - RIM
            if s > 0:
                value = pltpu.roll(jnp.where(row_of < s, halo, centre), LANES - s, 1)
            elif s < 0:
                value = pltpu.roll(jnp.where(row_of >= SIDE + s, halo, centre), -s, 1)
            else:
                value = centre
            pt_ref[a, at] = value

    def fill_step(w, carry):
        fill(RIM + w, ct_ref[w], ht_ref[w])
        return carry

    lax.fori_loop(0, SIDE, fill_step, 0, unroll=FILL_UNROLL)

    def window(g, blocks):
        return jnp.concatenate(
            [
                jnp.concatenate(
                    [
                        pt_ref[a, BLOCK * j : BLOCK * j + TAPW // GROUP, GROUP * g : GROUP * (g + 1)].reshape(
                            TAPW, LANES
                        )
                        for a in range(KS)
                    ],
                    axis=0,
                )
                for j in blocks
            ],
            axis=1,
        )

    def fold(values):
        total = values[:, :LANES]
        for j in range(1, values.shape[1] // LANES):
            total = total + values[:, LANES * j : LANES * (j + 1)]
        return total

    def work(blocks, defer):
        for g in range(GROUPS):
            out = mm(band_ref[g], window(g, blocks))
            for w in range(BLOCK):
                mixed_ref[w, GROUP * g : GROUP * (g + 1), : out.shape[1]] = out[GROUP * w : GROUP * (w + 1)]

        columns = [(w, j) for w in range(BLOCK) for j in blocks]
        steps = len(columns) // 4

        def pair_of(i):
            return columns[4 * i : 4 * (i + 1)]

        def gather(ref, i):
            return jnp.concatenate([ref[BLOCK * j + w] for w, j in pair_of(i)], axis=1)

        def front(i):
            tissue = gather(ts_ref, i)
            grad_out = gather(ut_ref, i).astype(F32) * (tissue * loss_factor)
            grad_branch = (grad_out * scale).astype(BF16)
            grad_active = mm(down_w, grad_branch)
            places = [(w, LANES * blocks.index(j)) for w, j in pair_of(i)]
            mixed = jnp.concatenate([mixed_ref[w, :, at : at + LANES] for w, at in places], axis=1)
            mean = jnp.sum(mixed, axis=0, keepdims=True) * (1.0 / C)
            centered = mixed - mean
            inverse = lax.rsqrt(jnp.sum(centered * centered, axis=0, keepdims=True) * (1.0 / C) + EPS)
            normed = centered * inverse
            lowered = (normed * gain).astype(BF16)
            hidden = mm(up_t, lowered)
            return tissue, grad_out, grad_branch, grad_active, normed, inverse, lowered, hidden

        def middle(state):
            grad_active, hidden = state[3], state[7]
            active, steepness = gelu_parts(hidden)
            return active.astype(BF16), (grad_active * steepness).astype(BF16)

        def large(state, pair):
            active, grad_hidden = pair
            acc_ref[0] += mm_nt(active, state[2])
            acc_ref[1] += mm_nt(grad_hidden, state[6])

        def back(i, state, pair):
            tissue, grad_out, _, _, normed, inverse, _, _ = state
            active, grad_hidden = pair
            grad_lowered = mm(up_w, grad_hidden)
            branch = mm(down_t, active)
            summed = gather(ct_ref, i).astype(F32) + scale * branch
            features = (summed * tissue).astype(BF16)
            gs_ref[...] += fold(grad_out * branch)
            gg_ref[...] += fold(grad_lowered * normed)
            scaled = grad_lowered * gain
            mean_one = jnp.sum(scaled, axis=0, keepdims=True) * (1.0 / C)
            mean_two = jnp.sum(scaled * normed, axis=0, keepdims=True) * (1.0 / C)
            grad_mixed = (inverse * (scaled - mean_one - normed * mean_two)).astype(BF16)
            for at, (w, j) in enumerate(pair_of(i)):
                lanes = slice(LANES * at, LANES * (at + 1))
                gm_ref[w, :, LANES * j : LANES * (j + 1)] = grad_mixed[:, lanes]
                ft_ref[BLOCK * j + w] = features[:, lanes]

        kept = []
        state = front(0)
        for i in range(steps):
            pair = middle(state)
            later = front(i + 1) if i + 1 < steps else None
            large(state, pair)
            if defer:
                kept.append((i, state, pair))
            else:
                back(i, state, pair)
            state = later

        def finish(some):
            for i in some:
                back(*kept[i])

        return finish

    work(tuple(range(1, BLOCKS - 1)), False)

    def gradient(g, blocks):
        left = jnp.concatenate(
            [
                jnp.concatenate(
                    [gm_ref[w, GROUP * g : GROUP * (g + 1), LANES * j : LANES * (j + 1)] for j in blocks],
                    axis=1,
                )
                for w in range(BLOCK)
            ],
            axis=0,
        )
        full = mm_nt(left, window(g, blocks))
        total = None
        for w in range(BLOCK):
            part = jnp.where(diagonal, full[GROUP * w : GROUP * (w + 1)], 0.0)
            if w:
                part = pltpu.roll(part, BAND - GROUP * w, 1)
            total = part if total is None else total + part
        return total


    for copy in sides_sent:
        copy.wait()
    for east in (0, 1):
        def rule(n, east=east):
            away = n // SLOTS - me
            away = away if east else -away
            return away * LANES + (n % SLOTS) * SIDE

        straight = spread(per_tile(2 + east, rule), 0)
        above = spread(per_tile(4 + east, rule), -1)
        below = spread(per_tile(6 + east, rule), 1)
        halo = jnp.where(top, above, jnp.where(bottom, below, -1))
        corner = REACH * LANES + SIDE * jnp.where(top, row_of - (SIDE - RIM), row_of)
        halo = jnp.where(halo >= REACH * LANES, corner, add_row(halo, row_of))
        index = jnp.concatenate([add_row(straight, row_of), halo], axis=1)
        select = onehot(iota(((REACH + 1) * LANES, 2 * LANES), 0) == index)
        first = 0 if east else SIDE - RIM
        base = 0 if east else REACH
        source = jnp.concatenate(
            [
                jnp.concatenate(
                    [ct_ref[first + i]]
                    + [recv_ref[base + d, i] for d in range(REACH - 1)]
                    + [pltpu.roll(strip_in[3 - east], (LANES - first - i) % LANES, 1)],
                    axis=1,
                )
                for i in range(RIM)
            ],
            axis=0,
        )
        sides = mm(source, select).astype(BF16)
        for i in range(RIM):
            side_ref[east * RIM + i] = sides[C * i : C * (i + 1)]

    for i in range(RIM):
        for east in (0, 1):
            both = side_ref[east * RIM + i]
            fill(east * (RIM + SIDE) + i, both[:, :LANES], both[:, LANES:])

    finish = work((0, BLOCKS - 1), True)

    lane_pad = jnp.zeros((HID, 128 - C), F32)
    row_pad = jnp.zeros((PIECE_PAD - PIECE, 128), F32)
    big_ref[...] = jnp.concatenate([acc_ref[1 - core], lane_pad], axis=1).astype(BF16)
    to_core = remote(big_ref, core_in, sum_send.at[0], sum_recv.at[0], partner)
    to_core.start()
    finish(range(1))

    to_core.wait()
    both = jnp.concatenate([acc_ref[core], lane_pad], axis=1) + core_in[...].astype(F32)
    for i in range(PLANE):
        piece = jnp.concatenate([both[PIECE * i : PIECE * (i + 1)], row_pad], axis=0)
        rs_src[i] = piece.astype(BF16)

    def scatter(target, source, at):
        for k in range(1, PLANE):
            i, device = plane_peer(k)
            remote(source(i), target(k), sum_send.at[at], sum_recv.at[at], device).start()

    def settle(ref, count, at):
        block = ref.at[pl.ds(0, count)]
        copy = remote(block, block, sum_send.at[at], sum_recv.at[at], partner)
        copy.wait()

    scatter(lambda k: rs_in.at[k], lambda i: rs_src.at[i], 1)
    finish(range(1, 2))

    totals = [gradient(g, range(BLOCKS)) for g in range(GROUPS)]
    totals = jnp.concatenate(totals, axis=0).astype(BF16)
    k_at, n_at = iota((BAND, LANES), 0), iota((BAND, LANES), 1)
    col_at = (k_at % TAPW) // GROUP
    place = onehot((col_at < KS) & (n_at == KS * (k_at // TAPW) + col_at))
    small = mm(totals, place)
    n_at = iota((C, LANES), 1)
    small = jnp.where(n_at == KS * KS, jnp.sum(gg_ref[...], axis=1, keepdims=True), small)
    small = jnp.where(n_at == KS * KS + 1, jnp.sum(gs_ref[...], axis=1, keepdims=True), small)
    small = jnp.concatenate([small[: C // 2, :64], small[C // 2 :, :64]], axis=1).astype(BF16)
    small_plane[me_plane] = small
    scatter(lambda k: small_plane.at[me_plane], lambda i: small_plane.at[me_plane], 3)

    settle(rs_in, PLANE - 1, 1)
    total = rs_src[me_plane].astype(F32)
    for k in range(1, PLANE):
        total = total + rs_in[k].astype(F32)
    y_buf[me_y] = total.astype(BF16)
    for k in range(1, 4):
        remote(y_buf.at[me_y], y_buf.at[me_y], sum_send.at[4], sum_recv.at[4], y_peer(k)).start()

    settle(small_plane, PLANE - 1, 3)
    total = small_plane[0].astype(F32)
    for k in range(1, PLANE):
        total = total + small_plane[k].astype(F32)
    at = 4 * core + me_y
    small_y[at] = total.astype(BF16)
    for device in column_peers:
        remote(small_y.at[at], small_y.at[at], sum_send.at[5], sum_recv.at[5], device).start()

    settle(y_buf, 3, 4)
    total = y_buf[0].astype(F32)
    for k in range(1, 4):
        total = total + y_buf[k].astype(F32)
    ag_buf[core, me_plane] = total.astype(BF16)
    mine = ag_buf.at[core, me_plane]
    for k in range(1, PLANE):
        remote(mine, mine, sum_send.at[6], gather_recv.at[k], plane_peer(k)[1]).start()
    remote(mine, mine, sum_send.at[7], sum_recv.at[7], partner).start()

    for w in range(0, SIDE, 4):
        part = jnp.concatenate([ft_ref[w + i] for i in range(4)], axis=0)
        feat_vmem[:, C * w : C * (w + 4)] = jnp.transpose(part)
    store = pltpu.make_async_copy(feat_vmem, feat_ref, local_sem.at[10])
    store.start()

    settle(small_y, 7, 5)
    total = small_y[0].astype(F32)
    for k in range(1, 8):
        total = total + small_y[k].astype(F32)
    small_ref[...] = total
    store_small = pltpu.make_async_copy(small_ref, small_out, local_sem.at[11])
    store_small.start()

    for k in range(1, PLANE):
        piece = ag_buf.at[core, lax.rem(me_plane + PLANE - k, PLANE)]
        remote(piece, piece, sum_send.at[6], gather_recv.at[k], partner).wait_recv()
        remote(piece, piece, sum_send.at[7], sum_recv.at[7], partner).start()
    sent = ag_buf.at[core, pl.ds(0, PLANE - 1)]
    remote(sent, sent, sum_send.at[6], sum_recv.at[6], partner).wait_send()
    other = ag_buf.at[1 - core]
    remote(other, other, sum_send.at[7], sum_recv.at[7], partner).wait()
    store_sums = pltpu.make_async_copy(ag_buf, ag_out, local_sem.at[12])
    store_sums.start()
    for copy in (store, store_small, store_sums):
        copy.wait()


def finish_kernel(*refs):
    inputs, outputs, refs = refs[:3], refs[3:9], refs[9:]
    (feat, ag_ref, small_ref), refs = refs[:3], refs[3:]
    (dw_ref, gain_ref, up_ref, down_ref, scale_ref), (sem_in, sem_out) = refs[:5], refs[5:]
    coming = [
        pltpu.make_async_copy(there, here, sem_in.at[i])
        for i, (there, here) in enumerate(zip(inputs, (feat, ag_ref, small_ref)))
    ]
    results = (feat, dw_ref, gain_ref, up_ref, down_ref, scale_ref)
    going = [
        pltpu.make_async_copy(here, there, sem_out.at[i])
        for i, (here, there) in enumerate(zip(results, outputs))
    ]
    for copy in coming:
        copy.start()
    coming[0].wait()
    going[0].start()
    coming[2].wait()
    total = small_ref[...]
    total = jnp.concatenate([total[:, :64], total[:, 64:]], axis=0)
    total = jnp.transpose(jnp.concatenate([total, jnp.zeros((C, 64), F32)], axis=1))
    dw_ref[...] = total[: KS * KS]
    gain_ref[...] = total[KS * KS : KS * KS + 1]
    scale_ref[...] = total[KS * KS + 1 : KS * KS + 2]
    for i in (1, 2, 5):
        going[i].start()
    coming[1].wait()
    for half, ref in ((0, down_ref), (1, up_ref)):
        joined = jnp.concatenate([ag_ref[half, i].astype(F32)[:PIECE] for i in range(PLANE)], axis=0)
        ref[...] = jnp.transpose(joined)[:C]
    for i in (3, 4):
        going[i].start()
    for copy in going:
        copy.wait()


def anywhere(count):
    return [pl.BlockSpec(memory_space=pl.ANY)] * count


def local(
    pixels,
    tissue,
    neighbours,
    upstream,
    stem_weight,
    stem_gain,
    dw_weight,
    norm_gain,
    up_weight,
    down_weight,
    layer_scale,
):
    tiles = lax.axis_size("tile")
    loss_factor = (tiles * lax.axis_size("slab") * SLOTS * SIDE * SIDE) ** (-0.5)
    dma = pltpu.SemaphoreType.DMA
    operands = (
        pixels[0],
        stem_weight,
        stem_gain[None],
        upstream.reshape(LANES, SIDE * C),
        tissue[0],
        dw_weight,
        norm_gain[None],
        up_weight,
        down_weight.T,
        layer_scale[None],
    )
    features, gathered, small = pl.pallas_call(
        functools.partial(whole_kernel, tiles, loss_factor),
        out_shape=(
            jax.ShapeDtypeStruct((LANES, SIDE * C), BF16),
            jax.ShapeDtypeStruct((2, PLANE, PIECE_PAD, 128), BF16),
            jax.ShapeDtypeStruct((C // 2, 128), F32),
        ),
        in_specs=[pl.BlockSpec(memory_space=pltpu.SMEM)] + anywhere(10),
        out_specs=tuple(anywhere(3)),
        scratch_shapes=[pltpu.VMEM(x.shape, x.dtype) for x in operands]
        + [
            pltpu.VMEM((LANES, SIDE * C), BF16),
            pltpu.VMEM((2, PLANE, PIECE_PAD, 128), BF16),
            pltpu.VMEM((C // 2, 128), F32),
            pltpu.VMEM((SIDE, C, LANES), BF16),
            pltpu.VMEM((2, C, LANES), BF16),
            pltpu.VMEM((4, C, LANES), BF16),
            pltpu.VMEM((2 * REACH, RIM, C, LANES), BF16),
            pltpu.VMEM((KS, PADW, C, LANES), BF16),
            pltpu.VMEM((SIDE, C, LANES), BF16),
            pltpu.VMEM((2 * RIM, C, 2 * LANES), BF16),
            pltpu.VMEM((GROUPS, BLOCK * GROUP, BAND), BF16),
            pltpu.VMEM((BLOCK, C, (BLOCKS - 2) * LANES), F32),
            pltpu.VMEM((BLOCK, C, BLOCKS * LANES), BF16),
            pltpu.VMEM((SIDE, C, LANES), BF16),
            pltpu.VMEM((SIDE, C, LANES), BF16),
            pltpu.VMEM((SIDE, 1, LANES), F32),
            pltpu.VMEM((2, HID, C), F32),
            pltpu.VMEM((C, LANES), F32),
            pltpu.VMEM((C, LANES), F32),
            pltpu.VMEM((HID, 128), BF16),
            pltpu.VMEM((HID, 128), BF16),
            pltpu.VMEM((PLANE, PIECE_PAD, 128), BF16),
            pltpu.VMEM((PLANE, PIECE_PAD, 128), BF16),
            pltpu.VMEM((4, PIECE_PAD, 128), BF16),
            pltpu.VMEM((PLANE, C // 2, 128), BF16),
            pltpu.VMEM((8, C // 2, 128), BF16),
            dma((2 * REACH + 2,)),
            dma((2 * REACH + 2,)),
            dma((8,)),
            dma((8,)),
            dma((PLANE,)),
            dma((13,)),
        ],
        compiler_params=pltpu.CompilerParams(
            collective_id=0, has_side_effects=True, vmem_limit_bytes=VMEM_BYTES
        ),
        name="whole",
    )(neighbours[0], *operands)
    features, grad_dw, grad_gain, grad_up, grad_down_t, grad_scale = pl.pallas_call(
        finish_kernel,
        out_shape=(
            jax.ShapeDtypeStruct((LANES, SIDE * C), BF16),
            jax.ShapeDtypeStruct((KS * KS, C), F32),
            jax.ShapeDtypeStruct((1, C), F32),
            jax.ShapeDtypeStruct((C, HID), F32),
            jax.ShapeDtypeStruct((C, HID), F32),
            jax.ShapeDtypeStruct((1, C), F32),
        ),
        in_specs=anywhere(3),
        out_specs=tuple(anywhere(6)),
        scratch_shapes=[
            pltpu.VMEM((LANES, SIDE * C), BF16),
            pltpu.VMEM((2, PLANE, PIECE_PAD, 128), BF16),
            pltpu.VMEM((C // 2, 128), F32),
            pltpu.VMEM((KS * KS, C), F32),
            pltpu.VMEM((1, C), F32),
            pltpu.VMEM((C, HID), F32),
            pltpu.VMEM((C, HID), F32),
            pltpu.VMEM((1, C), F32),
            dma((3,)),
            dma((6,)),
        ],
        compiler_params=pltpu.CompilerParams(vmem_limit_bytes=VMEM_BYTES),
        name="finish",
    )(features, gathered, small)
    return (
        features.reshape(upstream.shape),
        grad_dw,
        grad_gain[0],
        grad_up,
        grad_down_t.T,
        grad_scale[0],
    )


def solution(mesh):
    placed = (
        P("slab", "tile", None, None),
        P("slab", "tile", None),
        P("slab", "tile", None),
        P("slab", "tile", None, None),
        P(),
        P(),
        P(),
        P(),
        P(),
        P(),
        P(),
    )
    return jax.shard_map(
        local,
        mesh=mesh,
        in_specs=placed,
        out_specs=(P("slab", "tile", None, None), P(), P(), P(), P(), P()),
        check_vma=False,
    )
```
